128 devices in a mesh: fsdp: 8 (over z, x_hi), seq: 16 (over y, x_lo, core).
Axes of the slice: x: 4 (x_hi: 2, x_lo: 2; x = x_hi * 2 + x_lo), y: 4, z: 4, core: 2. Of those that a mesh axis runs over, the one named last changes fastest.
Arguments:
- tokens: bfloat16 [16384, 1024], P(('fsdp', 'seq')), may hold values from -6 to 6
- image_ids: int32 [16384], P(('fsdp', 'seq')), may hold values from 0 to 7, as said below
- valid: int32 [16384], P(('fsdp', 'seq')), may hold values from 0 to 1, as said below
- w_qkv: bfloat16 [1, 1024, 3072], P(None, 'fsdp'), may hold values from -0.1875 to 0.1875
- w_proj: bfloat16 [1, 1024, 1024], P(None, 'fsdp'), may hold values from -1.5 to 1.5
- w_fc1: bfloat16 [1, 1024, 4096], P(None, 'fsdp'), may hold values from -0.1875 to 0.1875
- w_fc2: bfloat16 [1, 4096, 1024], P(None, 'fsdp'), may hold values from -0.09375 to 0.09375
- norm_gain: bfloat16 [1, 2, 1024], P(None, None, 'fsdp'), may hold values from 0.5 to 1.5
- shifts: bfloat16 [1, 6, 1024], P(None, None, 'fsdp'), may hold values from -1.1953125 to 1.1953125
- layer_scale: bfloat16 [1, 2, 1024], P(None, None, 'fsdp'), may hold values from 0.29882812 to 1.1953125
- fc1_bias: bfloat16 [1, 4096], P(None, 'fsdp'), may hold values from -1.1953125 to 1.1953125
- grad_out: bfloat16 [16384, 1024], P(('fsdp', 'seq')), may hold values from -6 to 6
Outputs:
- result: bfloat16 [16384, 1024], P(('fsdp', 'seq'))
- grad_tokens: float32 [16384, 1024], P(('fsdp', 'seq'))
- grad_w_qkv: float32 [1, 1024, 3072], P(None, 'fsdp')
- grad_w_proj: float32 [1, 1024, 1024], P(None, 'fsdp')
- grad_w_fc1: float32 [1, 1024, 4096], P(None, 'fsdp')
- grad_w_fc2: float32 [1, 4096, 1024], P(None, 'fsdp')
- grad_norm_gain: float32 [1, 2, 1024], P(None, None, 'fsdp')
- grad_shifts: float32 [1, 6, 1024], P(None, None, 'fsdp')
- grad_layer_scale: float32 [1, 2, 1024], P(None, None, 'fsdp')
- grad_fc1_bias: float32 [1, 4096], P(None, 'fsdp')
The draws below stay inside these ranges and needn't reach their ends.
Inputs may be any that keep to these rules, and one draw needn't show every extreme that they name: `image_ids`: each window of 2048 consecutive tokens holds 2048 // 1370 whole images of exactly 1370 tokens each, their tokens at arbitrary positions of the window; every image has its own id, and the window's padding tokens carry the id of one of its images. `valid`: each window has exactly 2048 % 1370 padding tokens, at arbitrary positions.
All inputs are finite; a program needn't handle non-finite values.
Results may differ from the reference program's by a relative error of at most 0.022.
Values may be sent and summed in bfloat16 or wider, within the bound.
A program may use at most 128 MiB of HBM per device.

```python
import math
import jax
import jax.numpy as jnp
from jax import lax

D = 1024
HEADS = 16
HEAD_DIM = 64
FF = 4096
LAYERS = 1
IMAGE_TOK = 1370
GROUP_TOK = 2048
TOKENS = 16384


def group_layout(key):
    groups = TOKENS // GROUP_TOK
    per_group = GROUP_TOK // IMAGE_TOK
    base = jax.random.fold_in(key, 7)
    labels = jax.random.permutation(base, jnp.arange(groups * per_group, dtype=jnp.int32)).astype(jnp.int32)
    place_keys = jax.random.split(jax.random.fold_in(key, 13), groups)
    ranks = jax.vmap(lambda one_key: jax.random.permutation(one_key, jnp.arange(GROUP_TOK, dtype=jnp.int32)))(place_keys).astype(jnp.int32)
    local_id = jnp.minimum(ranks // IMAGE_TOK, per_group - 1)
    slot_id = local_id + per_group * jnp.arange(groups, dtype=jnp.int32)[:, None]
    global_id = jnp.take(labels, slot_id.reshape(TOKENS), axis=0)
    live = (ranks < per_group * IMAGE_TOK).astype(jnp.int32).reshape(TOKENS)
    return (global_id.astype(jnp.int32), live)


def draw_image_ids(key, part):
    return group_layout(key)[0]


def draw_valid(key, part):
    return group_layout(key)[1]


def block_levels(rng, shape, cuts, least, top_value):
    factor_of, own = 1.0, jax.random.fold_in(rng, 6)
    for position, parts in cuts:
        steps = jnp.exp(jax.random.uniform(jax.random.fold_in(own, position), (parts,), jnp.float32, least / len(cuts), top_value / len(cuts)))
        factor_of = factor_of * jnp.repeat(steps, shape[position] // parts).reshape([-1 if axis == position else 1 for axis in range(len(shape))])
    return factor_of


def gaussian(rng, dims, deviation, reach, cuts=(), held_as=jnp.bfloat16):
    array = jax.random.normal(rng, dims, jnp.float32) * deviation
    if len(cuts) > 0:
        array = block_levels(rng, dims, cuts, -0.22, 0.18) * array
    return jnp.clip(array, min=-reach, max=reach).astype(held_as)


def setup_inputs(seed: int = 0) -> dict:
    key_of = jax.random.split(jax.random.key(seed), 13)
    return {
        "tokens": gaussian(key_of[0], (TOKENS, D), 1.0, 6.0, ((0, 128),)),
        "image_ids": draw_image_ids(jax.random.fold_in(key_of[12], 71), 0),
        "valid": draw_valid(jax.random.fold_in(key_of[12], 71), 0),
        "w_qkv": gaussian(key_of[3], (LAYERS, D, 3 * D), D ** -0.5, 0.1875, ((1, 8),)),
        "w_proj": gaussian(key_of[4], (LAYERS, D, D), (D // 64) ** -0.5, 1.5, ((1, 8),)),
        "w_fc1": gaussian(key_of[5], (LAYERS, D, FF), D ** -0.5, 0.1875, ((1, 8),)),
        "w_fc2": gaussian(key_of[6], (LAYERS, FF, D), FF ** -0.5, 0.09375, ((1, 8),)),
        "norm_gain": jnp.clip(1.0 + 0.1 * jax.random.normal(key_of[7], (LAYERS, 2, D), jnp.float32), 0.5, 1.5).astype(jnp.bfloat16),
        "shifts": gaussian(key_of[8], (LAYERS, 6, D), 0.3, 1.1953125, ((2, 8),)),
        "layer_scale": jnp.clip(jnp.exp(math.log(1.1953125) - 1.3862944 * jax.random.uniform(key_of[9], (LAYERS, 2, D), jnp.float32) ** block_levels(key_of[9], (LAYERS, 2, D), ((2, 8),), -0.2, 0.2)), 0.29882812, 1.1953125).astype(jnp.bfloat16),
        "fc1_bias": gaussian(key_of[10], (LAYERS, FF), 0.3, 1.1953125, ((1, 8),)),
        "grad_out": gaussian(key_of[11], (TOKENS, D), 1.0, 6.0, ((0, 128),)),
    }


@jax.custom_vjp
def low(v):
    return lax.optimization_barrier(v.astype(jnp.bfloat16)).astype(jnp.float32)

@jax.custom_vjp
def low_back(v):
    return v

def low_keep(v):
    return (low(v), None)

def low_pass(kept, grad):
    return (grad,)

def back_keep(v):
    return (v, None)

def back_low(kept, grad):
    return (low(grad),)
low.defvjp(low_keep, low_pass)
low_back.defvjp(back_keep, back_low)

def matmul_hi(left, right):
    return jnp.dot(left, right, precision=lax.Precision.HIGHEST)

def layer_norm(values, gain, shift):
    mean_val = lax.optimization_barrier(jnp.mean(values, axis=-1, keepdims=True))
    centered = values - mean_val
    variance = lax.optimization_barrier(jnp.mean(centered * centered, axis=-1, keepdims=True))
    return centered * lax.rsqrt(variance + 1e-06) * gain + shift

def gelu_exact(pre_act):
    return 0.5 * pre_act * (1.0 + lax.erf(pre_act * 0.7071067811865476))

def attention_group(group_args):
    queries, key_rows, value_rows, group_ids, group_valid = group_args
    rows = queries.shape[0]
    query_h = queries.reshape(rows, HEADS, HEAD_DIM)
    key_h = key_rows.reshape(rows, HEADS, HEAD_DIM)
    value_h = value_rows.reshape(rows, HEADS, HEAD_DIM)
    allowed = (group_ids[:, None] == group_ids[None, :]) & (group_valid[None, :] == 1)
    raw = jnp.einsum('qhd,khd->hqk', query_h, key_h, precision=lax.Precision.HIGHEST)
    scores = low_back(raw) * HEAD_DIM ** (-0.5)
    scores = jnp.where(allowed[None], scores, -1e+30)
    row_max = lax.optimization_barrier(jnp.max(scores, axis=-1, keepdims=True))
    exp_terms = jnp.exp(scores - row_max)
    probs = low(exp_terms / lax.optimization_barrier(jnp.sum(exp_terms, axis=-1, keepdims=True)))
    mixed = jnp.einsum('hqk,khd->qhd', probs, value_h, precision=lax.Precision.HIGHEST)
    return mixed.reshape(rows, HEADS * HEAD_DIM)

def one_layer(residual, layer_params, ids_grouped, valid_grouped):
    wqkv, wproj, wfc1, wfc2, gains, shifts, scales, bias_one = layer_params
    groups = TOKENS // GROUP_TOK
    normed_in = low(layer_norm(residual, gains[0], shifts[0]))
    qkv_rows = matmul_hi(normed_in, wqkv)
    queries = low(low_back(qkv_rows[:, :D] + shifts[2]))
    key_rows = low(low_back(qkv_rows[:, D:2 * D]))
    value_rows = low(low_back(qkv_rows[:, 2 * D:] + shifts[3]))
    attn_groups = lax.map(jax.checkpoint(attention_group), (queries.reshape(groups, GROUP_TOK, D), key_rows.reshape(groups, GROUP_TOK, D), value_rows.reshape(groups, GROUP_TOK, D), ids_grouped, valid_grouped))
    attn_tok = low(low_back(attn_groups.reshape(TOKENS, D)))
    attn_branch = low_back(matmul_hi(attn_tok, wproj) + shifts[4])
    middle = residual + scales[0] * attn_branch
    normed_mid = low(layer_norm(middle, gains[1], shifts[1]))
    pre_act = low_back(matmul_hi(normed_mid, wfc1) + bias_one)
    act_vals = low(gelu_exact(pre_act))
    mlp_out = low_back(matmul_hi(act_vals, wfc2) + shifts[5])
    return middle + scales[1] * mlp_out

def reference(tokens, image_ids, valid, w_qkv, w_proj, w_fc1, w_fc2, norm_gain, shifts, layer_scale, fc1_bias, grad_out):
    groups = TOKENS // GROUP_TOK
    ids_grouped = image_ids.reshape(groups, GROUP_TOK)
    valid_grouped = valid.reshape(groups, GROUP_TOK)
    params = tuple((param.astype(jnp.float32) for param in (w_qkv, w_proj, w_fc1, w_fc2, norm_gain, shifts, layer_scale, fc1_bias)))
    start = tokens.astype(jnp.float32)

    def forward(residual, all_params):
        for layer_idx in range(LAYERS):
            residual = one_layer(residual, tuple((param[layer_idx] for param in all_params)), ids_grouped, valid_grouped)
        return residual
    final_res, pull = jax.vjp(forward, start, params)
    grad_start, grad_params = pull(grad_out.astype(jnp.float32))
    return (final_res.astype(jnp.bfloat16), grad_start, grad_params[0], grad_params[1], grad_params[2], grad_params[3], grad_params[4], grad_params[5], grad_params[6], grad_params[7])
```

```python
import functools

import jax
import jax.numpy as jnp
from jax import lax
from jax.experimental import pallas as pl
from jax.experimental.pallas import tpu as pltpu
from jax.sharding import PartitionSpec as P

NORM_EPS = 1e-06
NEG_FILL = -1e30
F32 = jnp.float32
BF16 = jnp.bfloat16
MESH = pl.DeviceIdType.MESH
NT = (((1,), (1,)), ((), ()))
TN = (((0,), (0,)), ((), ()))
NN = (((1,), (0,)), ((), ()))
VMEM_LIMIT = 60 * 1024 * 1024


def dot(left, right, dims=NN):
    return lax.dot_general(left, right, dims, preferred_element_type=F32)


class Place:
    def __init__(self):
        self.f = lax.axis_index("fsdp")
        self.s = lax.axis_index("seq")
        self.y = self.s // 4
        self.xl = (self.s // 2) % 2
        self.c = self.s % 2
        self.yp = (self.y + 1) % 4
        self.ym = (self.y + 3) % 4
        self.yo = (self.y + 2) % 4
        self.chip = self.s // 2
        self.j = self.y * 2 + self.c
        self.core = (self.f, self.slot(self.y, self.xl, 1 - self.c))
        self.xpart = (self.f, self.slot(self.y, 1 - self.xl, self.c))
        self.up = (self.f, self.slot(self.yp, self.xl, self.c))
        self.down = (self.f, self.slot(self.ym, self.xl, self.c))

    def slot(self, y, xl, c):
        return (y * 2 + xl) * 2 + c


def greet(me, seq=True, fsdp=True):
    barrier = pltpu.get_barrier_semaphore()
    count = 0
    if fsdp:
        for step in range(1, 8):
            pl.semaphore_signal(
                barrier, inc=1, device_id=((me.f + step) % 8, me.s), device_id_type=MESH
            )
        count += 7
    if seq:
        for step in range(1, 16):
            pl.semaphore_signal(
                barrier, inc=1, device_id=(me.f, (me.s + step) % 16), device_id_type=MESH
            )
        count += 15
    pl.semaphore_wait(barrier, count)


class Wire:
    def __init__(self, send_sem, recv_sem):
        self.send_sem, self.recv_sem = send_sem, recv_sem
        self.used = 0
        self.sent = []

    def send(self, src, dst, device):
        k = self.used
        self.used += 1
        copy = pltpu.make_async_remote_copy(
            src_ref=src,
            dst_ref=dst,
            send_sem=self.send_sem.at[k],
            recv_sem=self.recv_sem.at[k],
            device_id=device,
            device_id_type=MESH,
        )
        copy.start()
        self.sent.append(copy)
        return copy

    def drain(self):
        for copy in self.sent:
            copy.wait_send()
        self.sent = []


def to_fsdp(wire, me, src_of, dst_of):
    copies = []
    for step in range(1, 8):
        peer = (me.f + step) % 8
        copies.append(wire.send(src_of(peer), dst_of(me.f), (peer, me.s)))
    return copies


def arrived(copies):
    for copy in copies:
        copy.wait_recv()


class Gather8:
    def __init__(self, wire, me, ref):
        self.wire, self.me, self.ref = wire, me, ref
        self.half = ref.shape[1] // 2

    def slot(self, y, c=None):
        return y * 2 + (self.me.c if c is None else c)

    def start(self):
        w, me, r = self.wire, self.me, self.ref
        own = r.at[self.slot(me.y)]
        self.c_up = w.send(own, own, me.up)
        self.c_down = w.send(own, own, me.down)
        self.cores = [w.send(own, own, me.core)]

    def relay(self):
        w, me, r, h = self.wire, self.me, self.ref, self.half
        self.c_up.wait_recv()
        low = r.at[self.slot(me.ym)]
        head = r.at[self.slot(me.ym), pl.ds(0, h)]
        self.o_up = w.send(head, head, me.up)
        self.cores.append(w.send(low, low, me.core))
        self.c_down.wait_recv()
        high = r.at[self.slot(me.yp)]
        tail = r.at[self.slot(me.yp), pl.ds(h, h)]
        self.o_down = w.send(tail, tail, me.down)
        self.cores.append(w.send(high, high, me.core))

    def last(self):
        w, me, r = self.wire, self.me, self.ref
        self.o_up.wait_recv()
        self.o_down.wait_recv()
        far = r.at[self.slot(me.yo)]
        self.cores.append(w.send(far, far, me.core))

    def finish(self):
        arrived(self.cores)


class Gather16:
    def __init__(self, wire, me, ref):
        self.wire, self.me, self.ref = wire, me, ref
        self.half = ref.shape[1] // 2

    def slot(self, y, other=False):
        me = self.me
        return me.slot(y, 1 - me.xl if other else me.xl, me.c)

    def start(self):
        w, me, r = self.wire, self.me, self.ref
        own = r.at[self.slot(me.y)]
        self.cx = w.send(own, own, me.xpart)
        self.c_up = [w.send(own, own, me.up)]
        self.c_down = [w.send(own, own, me.down)]
        self.cores = [w.send(own, own, me.core)]

    def cross(self):
        w, me, r = self.wire, self.me, self.ref
        self.cx.wait_recv()
        part = r.at[self.slot(me.y, True)]
        self.c_up.append(w.send(part, part, me.up))
        self.c_down.append(w.send(part, part, me.down))
        self.cores.append(w.send(part, part, me.core))

    def relay(self, other):
        w, me, r, h = self.wire, self.me, self.ref, self.half
        self.c_up[int(other)].wait_recv()
        low = r.at[self.slot(me.ym, other)]
        head = r.at[self.slot(me.ym, other), pl.ds(0, h)]
        o_up = w.send(head, head, me.up)
        self.cores.append(w.send(low, low, me.core))
        self.c_down[int(other)].wait_recv()
        high = r.at[self.slot(me.yp, other)]
        tail = r.at[self.slot(me.yp, other), pl.ds(h, h)]
        o_down = w.send(tail, tail, me.down)
        self.cores.append(w.send(high, high, me.core))
        return o_up, o_down

    def last(self, pair, other):
        w, me, r = self.wire, self.me, self.ref
        arrived(pair)
        far = r.at[self.slot(me.yo, other)]
        self.cores.append(w.send(far, far, me.core))

    def run(self):
        self.cross()
        own = self.relay(False)
        part = self.relay(True)
        self.last(own, False)
        self.last(part, True)

    def finish(self):
        arrived(self.cores)


def full_row(params, row):
    return jnp.concatenate([params[f, row : row + 1, :] for f in range(8)], axis=1)


def norm_stats(values):
    mean_val = jnp.mean(values, axis=-1, keepdims=True)
    centered = values - mean_val
    variance = jnp.mean(centered * centered, axis=-1, keepdims=True)
    inverse = lax.rsqrt(variance + NORM_EPS)
    return centered * inverse, inverse


def head_half(me, rows128):
    return jnp.where(me.c == 0, rows128[:, :64], rows128[:, 64:])


def kernel_a(
    tok, gout, vin, pv, wq_in, wp_in, w1_in,
    nrm, grd, pv_all, wq_all, wp_all, w1_all, qa, ka, va, ow, at,
    v_all, om, ss, rs, as_, ar_,
):
    me = Place()
    wire = Wire(ss, rs)
    greet(me)
    pv_all[me.f] = pv[...]
    wq_all[me.f] = wq_in[...]
    wp_all[me.f] = wp_in[...]
    w1_all[me.f] = w1_in[...]
    v_all[me.s] = vin[...]
    got_pv = to_fsdp(wire, me, lambda p: pv, lambda f: pv_all.at[f])
    got_wq = to_fsdp(wire, me, lambda p: wq_in, lambda f: wq_all.at[f])
    normed, _ = norm_stats(tok[...].astype(F32))
    arrived(got_pv)
    params = pv_all[...].astype(F32)
    nrm[me.s] = (normed * full_row(params, 0) + full_row(params, 2)).astype(BF16)
    gather = Gather16(wire, me, nrm)
    gather.start()
    got_v = []
    for step in range(1, 16):
        peer = (me.s + step) % 16
        got_v.append(wire.send(vin, v_all.at[me.s], (me.f, peer)))
    grd[me.j] = (full_row(params, 9) * gout[...].astype(F32)).astype(BF16)
    gather.run()
    grad_gather = Gather8(wire, me, grd)
    grad_gather.start()
    half = pl.ds(pl.multiple_of(me.c * 64, 64), 64)
    got_wp = to_fsdp(wire, me, lambda p: wp_in.at[half], lambda f: wp_all.at[f, half])
    got_w1 = to_fsdp(wire, me, lambda p: w1_in, lambda f: w1_all.at[f])

    arrived(got_v)
    flags = v_all[:, 0, :].astype(F32)
    flags = jnp.concatenate([flags, jnp.zeros((112, 128), F32)], axis=0).T
    ext_lane = lax.broadcasted_iota(jnp.int32, (128, 64), 1)
    q_ext = jnp.where(ext_lane == 0, 1.0, 0.0).astype(BF16)
    v_ext = jnp.where(ext_lane < 3, 1.0, 0.0).astype(BF16)
    for blk in range(16):
        bias = (1.0 - flags[:, blk : blk + 1]) * NEG_FILL
        ext = jnp.where(ext_lane == 0, bias, jnp.where(ext_lane < 4, 1.0, 0.0))
        ka[blk * 128 : (blk + 1) * 128, 64:] = ext.astype(BF16)
    bias_rows = head_half(me, pv_all[me.s // 2].astype(F32))
    bias_q, bias_v = bias_rows[4:5, :], bias_rows[5:6, :]
    gather.finish()
    arrived(got_wq)
    wq = wq_all[...].reshape(1024, 256)

    def project(blk, carry):
        qkv = dot(nrm[blk], wq)
        rows = pl.ds(pl.multiple_of(blk * 128, 128), 128)
        query = ((qkv[:, :64] + bias_q).astype(BF16) * 0.125).astype(BF16)
        qa[rows, :] = jnp.concatenate([query, q_ext], axis=1)
        ka[rows, :64] = qkv[:, 64:128].astype(BF16)
        value = (qkv[:, 128:192] + bias_v).astype(BF16)
        va[rows, :] = jnp.concatenate([value, v_ext], axis=1)
        return carry

    lax.fori_loop(0, 16, project, 0)
    grad_gather.relay()

    def message(k, e):
        blk = ((me.chip + 1 + k) % 8) * 2 + e
        return pltpu.make_async_remote_copy(
            src_ref=om.at[blk],
            dst_ref=at.at[me.s],
            send_sem=as_.at[2 * k + e],
            recv_sem=ar_.at[2 * k + me.c],
            device_id=(me.f, blk),
            device_id_type=MESH,
        )

    out_lane = lax.broadcasted_iota(jnp.int32, (256, 128), 1)

    def attend(k):
        chip = (me.chip + 1 + k) % 8
        rows = pl.ds(pl.multiple_of(chip * 256, 256), 256)
        scores = dot(qa[rows, :], ka[...], NT)
        row_max = jnp.max(scores, axis=1, keepdims=True)
        terms = jnp.exp(scores - row_max).astype(BF16)
        mixed = dot(terms, va[...])
        total = mixed[:, 64:65]
        heads = mixed / total
        log_sum = row_max + jnp.log(total)
        ow[rows, :] = jnp.where(out_lane < 64, heads, log_sum)
        rounded = heads[:, :64].astype(BF16)
        for e in range(2):
            piece = rounded[e * 128 : (e + 1) * 128]
            om[chip * 2 + e] = jnp.concatenate([piece[:64], piece[64:]], axis=1)

    def step(k, carry):
        attend(k)
        message(k, 0).start()
        message(k, 1).start()
        return carry

    lax.fori_loop(0, 4, step, 0)
    grad_gather.last()
    lax.fori_loop(4, 7, step, 0)
    attend(7)
    at[me.s] = om[me.s]
    partner = wire.send(om.at[me.s + 1 - 2 * me.c], at.at[me.s], me.core)

    def collect(k, carry):
        for e in range(2):
            copy = message(k, e)
            copy.wait_send()
            src = ((me.chip + 7 - k) % 8) * 2 + e
            pltpu.make_async_remote_copy(
                src_ref=om.at[src],
                dst_ref=at.at[src],
                send_sem=as_.at[2 * k + e],
                recv_sem=ar_.at[2 * k + e],
                device_id=(me.f, src),
                device_id_type=MESH,
            ).wait_recv()
        return carry

    lax.fori_loop(0, 7, collect, 0)
    partner.wait_recv()
    arrived(got_wp)
    swap = []
    for f in range(8):
        swap.append(wire.send(wp_all.at[f, half], wp_all.at[f, half], me.core))
    grad_gather.finish()
    arrived(got_w1)
    arrived(swap)
    wire.drain()


def vmem(count):
    return [pl.BlockSpec(memory_space=pltpu.VMEM)] * count


def sds(shape, dtype):
    return jax.ShapeDtypeStruct(shape, dtype)


def call_a(*args):
    outs = (
        sds((16, 128, 1024), BF16),
        sds((8, 128, 1024), BF16),
        sds((8, 16, 128), BF16),
        sds((8, 128, 256), BF16),
        sds((8, 128, 1024), BF16),
        sds((8, 128, 512), BF16),
        sds((2048, 128), BF16),
        sds((2048, 128), BF16),
        sds((2048, 128), BF16),
        sds((2048, 128), F32),
        sds((16, 64, 128), BF16),
    )
    return pl.pallas_call(
        kernel_a,
        out_shape=outs,
        in_specs=vmem(len(args)),
        out_specs=vmem(len(outs)),
        scratch_shapes=[
            pltpu.VMEM((16, 16, 128), BF16),
            pltpu.VMEM((16, 64, 128), BF16),
            pltpu.SemaphoreType.DMA((96,)),
            pltpu.SemaphoreType.DMA((96,)),
            pltpu.SemaphoreType.DMA((14,)),
            pltpu.SemaphoreType.DMA((14,)),
        ],
        name="front",
        compiler_params=pltpu.CompilerParams(
            collective_id=1, has_side_effects=True, vmem_limit_bytes=VMEM_LIMIT
        ),
    )(*args)


class ReduceY:
    def __init__(self, wire, me, part, slot, from_core, from_far, from_near):
        self.wire, self.me, self.part, self.slot = wire, me, part, slot
        self.from_core, self.from_far, self.from_near = from_core, from_far, from_near
        self.order = (me.yo, me.yp, me.ym, me.y)

    def start(self):
        me = self.me
        self.cores = []
        for d, y in enumerate(self.order):
            src = self.part.at[self.slot(y, 1 - me.c)]
            self.cores.append(self.wire.send(src, self.from_core.at[d], me.core))

    def combine(self, d):
        self.cores[d].wait_recv()
        own = self.part[self.slot(self.order[d], self.me.c)]
        total = own.astype(F32) + self.from_core[d].astype(F32)
        self.from_core[d] = total.astype(BF16)

    def far(self):
        w, me, acc = self.wire, self.me, self.from_core
        h = acc.shape[1] // 2
        self.head, self.tail = pl.ds(0, h), pl.ds(h, h)
        self.combine(0)
        self.f_up = w.send(acc.at[0, self.head], self.from_far.at[0], me.up)
        self.f_down = w.send(acc.at[0, self.tail], self.from_far.at[1], me.down)
        self.combine(1)
        self.n_up = [w.send(acc.at[1, self.tail], self.from_near.at[0, self.tail], me.up)]
        self.combine(2)
        self.n_down = [w.send(acc.at[2, self.head], self.from_near.at[1, self.head], me.down)]

    def near(self):
        w, me, acc = self.wire, self.me, self.from_core
        self.f_up.wait_recv()
        total = acc[1, self.head].astype(F32) + self.from_far[0].astype(F32)
        acc[1, self.head] = total.astype(BF16)
        self.n_up.append(w.send(acc.at[1, self.head], self.from_near.at[0, self.head], me.up))
        self.f_down.wait_recv()
        total = acc[2, self.tail].astype(F32) + self.from_far[1].astype(F32)
        acc[2, self.tail] = total.astype(BF16)
        self.n_down.append(w.send(acc.at[2, self.tail], self.from_near.at[1, self.tail], me.down))

    def result(self):
        self.cores[3].wait_recv()
        own = self.part[self.slot(self.me.y, self.me.c)]
        total = own.astype(F32) + self.from_core[3].astype(F32)
        arrived(self.n_up)
        arrived(self.n_down)
        return total + self.from_near[0].astype(F32) + self.from_near[1].astype(F32)


def norm_back(cotangent, gain, normed, inverse):
    scaled = cotangent * gain
    first = jnp.mean(scaled, axis=-1, keepdims=True)
    second = jnp.mean(scaled * normed, axis=-1, keepdims=True)
    return inverse * (scaled - first - normed * second)


def column_sum(values):
    return jnp.sum(values, axis=0, keepdims=True)


def kernel_b(
    tok, gout, pv_all, at, wp_in, w1_in, w2_in, grd,
    mid, gmid, atg, mp, dw1, dw2, gh, gac, vec, db1,
    w2_all, nmg, act, gpre, gn, r_core, r_far, r_near, msg, gat, ss, rs,
):
    me = Place()
    wire = Wire(ss, rs)
    greet(me)
    mine = pl.ds(pl.multiple_of(me.j * 64, 64), 64)
    w2_all[me.f] = w2_in[mine]
    got_w2 = to_fsdp(wire, me, lambda p: w2_in.at[mine], lambda f: w2_all.at[f])
    params = pv_all[...].astype(F32)
    heads = [jnp.concatenate([at[h, :, :64], at[h, :, 64:]], axis=0) for h in range(16)]
    attn_tok = jnp.concatenate(heads, axis=1)
    atg[me.j] = attn_tok
    wp = wp_in[...].reshape(1024, 1024)
    branch = dot(attn_tok, wp) + full_row(params, 6)
    middle = tok[...].astype(F32) + full_row(params, 8) * branch
    mid[...] = middle
    normed, inverse = norm_stats(middle)
    gain = full_row(params, 1)
    nmg[me.j] = (normed * gain + full_row(params, 3)).astype(BF16)
    gather = Gather8(wire, me, nmg)
    gather.start()
    gather.relay()
    attn_gather = Gather8(wire, me, atg)
    attn_gather.start()
    gather.last()
    gather.finish()
    arrived(got_w2)
    bias_one = jnp.concatenate([params[f, 10:11, :64] for f in range(8)], axis=1)

    def feed(b, carry):
        two = pl.ds(2 * b, 2)
        rows = pl.ds(pl.multiple_of(b * 256, 256), 256)
        w1 = w1_in[...].reshape(1024, 512)
        w2 = w2_all[...].reshape(512, 1024)
        pre = dot(nmg[two].reshape(256, 1024), w1) + bias_one
        cdf = 0.5 * (1.0 + lax.erf(pre * 0.7071067811865476))
        acts = (pre * cdf).astype(BF16)
        act[rows, :] = acts
        mp[two] = dot(acts, w2).astype(BF16).reshape(2, 128, 1024)
        grad_act = dot(grd[two].reshape(256, 1024), w2, NT)
        slope = cdf + pre * jnp.exp(-0.5 * pre * pre) * 0.3989422804014327
        grad_pre = (grad_act * slope).astype(BF16)
        gpre[rows, :] = grad_pre
        gn[two] = dot(grad_pre, w1, NT).astype(BF16).reshape(2, 128, 1024)
        return carry + column_sum(grad_pre.astype(F32))

    attn_gather.relay()
    db1[...] = lax.fori_loop(0, 4, feed, jnp.zeros((1, 512), F32))
    slot = lambda y, c: y * 2 + c
    reduce = ReduceY(wire, me, gn, slot, r_core, r_far, r_near)
    reduce.start()
    reduce.far()
    attn_gather.last()
    dw2[...] = dot(act[...], grd[...].reshape(1024, 1024), TN).astype(BF16).reshape(8, 64, 1024)
    reduce.near()
    dw1[...] = dot(nmg[...].reshape(1024, 1024), gpre[...], TN).astype(BF16).reshape(8, 128, 512)
    cotangent = reduce.result()
    grad_middle = gout[...].astype(F32) + norm_back(cotangent, gain, normed, inverse)
    gmid[...] = grad_middle
    grad_attn = (full_row(params, 8) * grad_middle).astype(BF16)
    gat[...] = grad_attn
    grad_tok = dot(grad_attn, wp, NT).astype(BF16)
    for h in range(16):
        piece = grad_tok[:, h * 64 : (h + 1) * 64]
        msg[h] = jnp.concatenate([piece[:64], piece[64:]], axis=1)
    gh[me.s] = msg[me.s]
    copies = []
    for step in range(1, 16):
        peer = (me.s + step) % 16
        copies.append(wire.send(msg.at[peer], gh.at[me.s], (me.f, peer)))
    for step in range(1, 8):
        peer = (me.j + step) % 8
        cols = pl.ds(pl.multiple_of(peer * 128, 128), 128)
        device = (me.f, me.slot(peer // 2, me.xl, peer % 2))
        copies.append(wire.send(gat.at[:, cols], gac.at[me.j], device))
    gac[me.j] = gat[:, pl.ds(pl.multiple_of(me.j * 128, 128), 128)]
    zero = jnp.zeros((1, 1024), F32)
    rows = [
        zero,
        column_sum(cotangent * normed),
        zero,
        column_sum(cotangent),
        zero,
        zero,
        column_sum(grad_attn.astype(F32)),
        column_sum(grd[me.j].astype(F32)),
        column_sum(grad_middle * branch),
        jnp.zeros((7, 1024), F32),
    ]
    vec[...] = jnp.concatenate(rows, axis=0)
    attn_gather.finish()
    arrived(copies)
    wire.drain()


def call_b(*args):
    outs = (
        sds((128, 1024), F32),
        sds((128, 1024), F32),
        sds((8, 128, 1024), BF16),
        sds((8, 128, 1024), BF16),
        sds((8, 128, 512), BF16),
        sds((8, 64, 1024), BF16),
        sds((16, 64, 128), BF16),
        sds((8, 128, 128), BF16),
        sds((16, 1024), F32),
        sds((1, 512), F32),
    )
    return pl.pallas_call(
        kernel_b,
        out_shape=outs,
        in_specs=vmem(len(args)),
        out_specs=vmem(len(outs)),
        scratch_shapes=[
            pltpu.VMEM((8, 64, 1024), BF16),
            pltpu.VMEM((8, 128, 1024), BF16),
            pltpu.VMEM((1024, 512), BF16),
            pltpu.VMEM((1024, 512), BF16),
            pltpu.VMEM((8, 128, 1024), BF16),
            pltpu.VMEM((4, 128, 1024), BF16),
            pltpu.VMEM((2, 64, 1024), BF16),
            pltpu.VMEM((2, 128, 1024), BF16),
            pltpu.VMEM((16, 64, 128), BF16),
            pltpu.VMEM((128, 1024), BF16),
            pltpu.SemaphoreType.DMA((96,)),
            pltpu.SemaphoreType.DMA((96,)),
        ],
        name="middle",
        compiler_params=pltpu.CompilerParams(
            collective_id=2, has_side_effects=True, vmem_limit_bytes=VMEM_LIMIT
        ),
    )(*args)


def three_parts(values):
    first = values.astype(BF16)
    rest = values - first.astype(F32)
    second = rest.astype(BF16)
    third = (rest - second.astype(F32)).astype(BF16)
    return first, second, third


def kernel_c(
    tok, gout, pv_all, wq_all, nrm, qa, ka, va, ow, gh, mid, gmid, atg, mp, dw1, dw2, gac, vecb, db1,
    res, gtok, o_qkv, o_proj, o_fc1, o_fc2, o_vec,
    ga, qb, kt, dk, dv, dq, pn, m_core, m_far, m_near,
    c_own, f_own, n_own, c_oth, f_oth, n_oth, x_sum, x_in,
    dwp, r1, r2, rp, x1, x2, xp, g1, g2, gp, dwq, rq, gq, vs, vr, vq, ss, rs,
):
    me = Place()
    wire = Wire(ss, rs)
    greet(me)
    params = pv_all[...].astype(F32)
    slot = lambda y, c: y * 2 + c
    mlp = ReduceY(wire, me, mp, slot, m_core, m_far, m_near)
    mlp.start()
    got = to_fsdp(wire, me, lambda p: dw1.at[p], lambda f: r1.at[f])
    got += to_fsdp(wire, me, lambda p: dw2.at[p], lambda f: r2.at[f])
    proj_cols = gac[...].reshape(1024, 128)
    dwp[...] = dot(atg[...].reshape(1024, 1024), proj_cols, TN).astype(BF16).reshape(8, 128, 128)
    got += to_fsdp(wire, me, lambda p: dwp.at[p], lambda f: rp.at[f])
    r1[me.f] = dw1[me.f]
    r2[me.f] = dw2[me.f]
    rp[me.f] = dwp[me.f]

    lane = lax.broadcasted_iota(jnp.int32, (128, 128), 1)
    for blk in range(16):
        rows = slice(blk * 128, (blk + 1) * 128)
        packed = gh[blk]
        grad = jnp.concatenate([packed[:, :64], packed[:, 64:]], axis=0)
        heads = ow[rows, :]
        delta = jnp.sum(grad.astype(F32) * heads[:, :64], axis=1, keepdims=True)
        d1, d2, d3 = three_parts(-delta)
        l1, l2, l3 = three_parts(-heads[:, 64:65])
        wide = jnp.concatenate([grad, jnp.zeros((128, 64), BF16)], axis=1).astype(F32)
        wide = jnp.where(lane == 64, d1.astype(F32), wide)
        wide = jnp.where(lane == 65, d2.astype(F32), wide)
        wide = jnp.where(lane == 66, d3.astype(F32), wide)
        ga[rows, :] = wide.astype(BF16)
        wide = qa[rows, :].astype(F32)
        wide = jnp.where(lane == 65, l1.astype(F32), wide)
        wide = jnp.where(lane == 66, l2.astype(F32), wide)
        wide = jnp.where(lane == 67, l3.astype(F32), wide)
        qb[rows, :] = wide.astype(BF16)
        kt[:, rows] = ka[rows, :].astype(F32).T.astype(BF16)
    dk[...] = jnp.zeros_like(dk)
    dv[...] = jnp.zeros_like(dv)
    mlp.far()

    def back(b, carry):
        rows = pl.ds(pl.multiple_of(b * 256, 256), 256)
        query, grad = qb[rows, :], ga[rows, :]
        probs = jnp.exp(dot(ka[...], query, NT))
        dv[...] += dot(probs.astype(BF16), grad)
        slope = dot(va[...], grad, NT)
        scores = (probs * slope).astype(BF16)
        dk[...] += dot(scores, query)
        turned = dot(kt[...], scores)
        dq[rows, :64] = (turned.T[:, :64] * 0.125).astype(BF16)
        return carry

    lax.fori_loop(0, 4, back, 0)
    mlp.near()
    lax.fori_loop(4, 8, back, 0)
    dq[:, 64:128] = dk[:, :64].astype(BF16)
    dq[:, 128:] = jnp.concatenate(
        [dv[:, :64].astype(BF16), jnp.zeros((2048, 64), BF16)], axis=1
    )

    def spread(blk, carry):
        rows = pl.ds(pl.multiple_of(blk * 128, 128), 128)
        wq = wq_all[...].reshape(1024, 256)
        pn[blk] = dot(dq[rows, :], wq, NT).astype(BF16)
        return carry

    lax.fori_loop(0, 16, spread, 0)
    others = ReduceY(
        wire, me, pn, lambda y, c: me.slot(y, 1 - me.xl, c), c_oth, f_oth, n_oth
    )
    owns = ReduceY(wire, me, pn, lambda y, c: me.slot(y, me.xl, c), c_own, f_own, n_own)
    others.start()
    owns.start()
    others.far()
    owns.far()

    grad_wq = dot(nrm[...].reshape(2048, 1024), dq[...], TN)
    dwq[...] = grad_wq.astype(BF16).reshape(8, 128, 256)
    rq[me.f] = dwq[me.f]
    got_q = to_fsdp(wire, me, lambda p: dwq.at[p], lambda f: rq.at[f])

    sums = column_sum(dq[...].astype(F32))
    mlp_out = mlp.result() + full_row(params, 7)
    res[...] = (mid[...] + full_row(params, 9) * mlp_out).astype(BF16)
    grad_scale = column_sum(gout[...].astype(F32) * mlp_out)
    vec = vecb[...]
    head_at = me.s // 2
    zero64 = jnp.zeros((1, 64), F32)
    for f in range(8):
        w_blk = wq_all[f].astype(F32)
        first = jnp.sum(w_blk * grad_wq[f * 128 : (f + 1) * 128], axis=1, keepdims=True)
        second = jnp.sum(w_blk * sums, axis=1, keepdims=True)
        turned = jnp.where(lane == 0, first, jnp.where(lane == 1, second, 0.0)).T
        total = turned[1:2]
        gain = (turned[0:1] - params[f, 2:3] * total) / params[f, 0:1]
        cols = slice(f * 128, (f + 1) * 128)
        placed = []
        for part in (sums[:, :64], sums[:, 128:192]):
            pair = jnp.where(
                me.c == 0,
                jnp.concatenate([part, zero64], axis=1),
                jnp.concatenate([zero64, part], axis=1),
            )
            placed.append(jnp.where(head_at == f, pair, 0.0))
        piece = db1[:, f * 64 : (f + 1) * 64]
        pair = jnp.where(
            me.c == 0,
            jnp.concatenate([piece, zero64], axis=1),
            jnp.concatenate([zero64, piece], axis=1),
        )
        bias = [jnp.where(me.y == row, pair, 0.0) for row in range(4)]
        vs[f] = jnp.concatenate(
            [
                gain,
                vec[1:2, cols],
                total,
                vec[3:4, cols],
                placed[0],
                placed[1],
                vec[6:9, cols],
                grad_scale[:, cols],
                *bias,
                jnp.zeros((2, 128), F32),
            ],
            axis=0,
        )
    vr[me.f] = vs[me.f]
    got_v = to_fsdp(wire, me, lambda p: vs.at[p], lambda f: vr.at[f])
    others.near()
    owns.near()

    arrived(got)

    def eight(ref):
        total = ref[0].astype(F32)
        for f in range(1, 8):
            total = total + ref[f].astype(F32)
        return total.astype(BF16)

    x1[0] = eight(r1)
    x2[0] = eight(r2)
    xp[0] = eight(rp)
    swap = [wire.send(x.at[0], x.at[1], me.xpart) for x in (x1, x2, xp)]

    x_sum[...] = others.result().astype(BF16)
    crossed = wire.send(x_sum, x_in, me.xpart)

    arrived(got_q)
    gq[me.s] = eight(rq)
    gather_q = Gather16(wire, me, gq)
    gather_q.start()
    arrived(got_v)
    total = vr[0]
    for f in range(1, 8):
        total = total + vr[f]
    vq[me.s] = total
    got_vq = []
    for step in range(1, 16):
        got_vq.append(wire.send(vq.at[me.s], vq.at[me.s], (me.f, (me.s + step) % 16)))

    arrived(swap)
    gathers = []
    for x, g in ((x1, g1), (x2, g2), (xp, gp)):
        g[me.j] = (x[0].astype(F32) + x[1].astype(F32)).astype(BF16)
        gathers.append(Gather8(wire, me, g))
    for gather in gathers:
        gather.start()
    cotangent = owns.result()
    gather_q.run()
    for gather in gathers:
        gather.relay()
    normed, inverse = norm_stats(tok[...].astype(F32))
    crossed.wait_recv()
    cotangent = cotangent + x_in[...].astype(F32)
    gtok[...] = gmid[...] + norm_back(cotangent, full_row(params, 0), normed, inverse)
    for gather in gathers:
        gather.last()
    gather_q.finish()
    for part in range(3):
        cols = slice(part * 64, (part + 1) * 64)
        for k in range(8):
            pair = jnp.concatenate([gq[2 * k, :, cols], gq[2 * k + 1, :, cols]], axis=1)
            o_qkv[:, part * 1024 + k * 128 : part * 1024 + (k + 1) * 128] = pair.astype(F32)
    for gather in gathers:
        gather.finish()
    for j in range(8):
        o_proj[:, j * 128 : (j + 1) * 128] = gp[j].astype(F32)
        o_fc2[j] = g2[j].astype(F32)
    for f in range(8):
        cols = slice(f * 64, (f + 1) * 64)
        for k in range(4):
            pair = jnp.concatenate([g1[2 * k, :, cols], g1[2 * k + 1, :, cols]], axis=1)
            o_fc1[:, f * 512 + k * 128 : f * 512 + (k + 1) * 128] = pair.astype(F32)
    arrived(got_vq)
    total = vq[0]
    for s in range(1, 16):
        total = total + vq[s]
    o_vec[...] = total
    wire.drain()


def call_c(*args):
    outs = (
        sds((128, 1024), BF16),
        sds((128, 1024), F32),
        sds((128, 3072), F32),
        sds((128, 1024), F32),
        sds((128, 4096), F32),
        sds((8, 64, 1024), F32),
        sds((16, 128), F32),
    )
    block = (128, 1024)
    reduce = [
        pltpu.VMEM((4, *block), BF16),
        pltpu.VMEM((2, 64, 1024), BF16),
        pltpu.VMEM((2, *block), BF16),
    ]
    return pl.pallas_call(
        kernel_c,
        out_shape=outs,
        in_specs=vmem(len(args)),
        out_specs=vmem(len(outs)),
        scratch_shapes=[
            pltpu.VMEM((2048, 128), BF16),
            pltpu.VMEM((2048, 128), BF16),
            pltpu.VMEM((128, 2048), BF16),
            pltpu.VMEM((2048, 128), F32),
            pltpu.VMEM((2048, 128), F32),
            pltpu.VMEM((2048, 256), BF16),
            pltpu.VMEM((16, *block), BF16),
            *reduce,
            *reduce,
            *reduce,
            pltpu.VMEM(block, BF16),
            pltpu.VMEM(block, BF16),
            pltpu.VMEM((8, 128, 128), BF16),
            pltpu.VMEM((8, 128, 512), BF16),
            pltpu.VMEM((8, 64, 1024), BF16),
            pltpu.VMEM((8, 128, 128), BF16),
            pltpu.VMEM((2, 128, 512), BF16),
            pltpu.VMEM((2, 64, 1024), BF16),
            pltpu.VMEM((2, 128, 128), BF16),
            pltpu.VMEM((8, 128, 512), BF16),
            pltpu.VMEM((8, 64, 1024), BF16),
            pltpu.VMEM((8, 128, 128), BF16),
            pltpu.VMEM((8, 128, 256), BF16),
            pltpu.VMEM((8, 128, 256), BF16),
            pltpu.VMEM((16, 128, 256), BF16),
            pltpu.VMEM((8, 16, 128), F32),
            pltpu.VMEM((8, 16, 128), F32),
            pltpu.VMEM((16, 16, 128), F32),
            pltpu.SemaphoreType.DMA((192,)),
            pltpu.SemaphoreType.DMA((192,)),
        ],
        name="back",
        compiler_params=pltpu.CompilerParams(
            collective_id=3, has_side_effects=True, vmem_limit_bytes=VMEM_LIMIT
        ),
    )(*args)


def pick_params(norm_gain, shifts, layer_scale, fc1_bias, j):
    bias = lax.dynamic_index_in_dim(fc1_bias[0].reshape(8, 64), j, 0)
    bias = jnp.pad(bias, ((0, 0), (0, 64)))
    return jnp.concatenate(
        [norm_gain[0], shifts[0], layer_scale[0], bias, jnp.zeros((5, 128), BF16)], axis=0
    )


def body(
    tokens, image_ids, valid, w_qkv, w_proj, w_fc1, w_fc2,
    norm_gain, shifts, layer_scale, fc1_bias, grad_out,
):
    s = lax.axis_index("seq")
    j = (s // 4) * 2 + s % 2
    pv = pick_params(norm_gain, shifts, layer_scale, fc1_bias, j)
    vin = jnp.broadcast_to(valid.astype(BF16)[None, :], (16, 128))
    wq = lax.dynamic_index_in_dim(w_qkv[0].reshape(128, 3, 16, 64), s, 2, keepdims=False)
    wq = jnp.pad(wq.reshape(128, 192), ((0, 0), (0, 64)))
    w1 = lax.dynamic_index_in_dim(w_fc1[0].reshape(128, 8, 8, 64), j, 2, keepdims=False)
    w1 = w1.reshape(128, 512)
    nrm, grd, pv_all, wq_all, wp_all, w1_all, qa, ka, va, ow, at = call_a(
        tokens, grad_out, vin, pv, wq, w_proj[0], w1
    )
    mid, gmid, atg, mp, dw1, dw2, gh, gac, vec, db1 = call_b(
        tokens, grad_out, pv_all, at, wp_all, w1_all, w_fc2[0], grd
    )
    res, gtok, g_qkv, g_proj, g_fc1, g_fc2, g_vec = call_c(
        tokens, grad_out, pv_all, wq_all, nrm, qa, ka, va, ow, gh,
        mid, gmid, atg, mp, dw1, dw2, gac, vec, db1,
    )
    return (
        res,
        gtok,
        g_qkv[None],
        g_proj[None],
        g_fc1[None],
        g_fc2.reshape(1, 512, 1024),
        g_vec[None, 0:2],
        g_vec[None, 2:8],
        g_vec[None, 8:10],
        g_vec[10:14].reshape(1, 512),
    )


def solution(mesh):
    rows = P(("fsdp", "seq"), None)
    flat = P(("fsdp", "seq"))
    mats = P(None, "fsdp", None)
    vecs = P(None, None, "fsdp")
    bias = P(None, "fsdp")
    return jax.shard_map(
        body,
        mesh=mesh,
        in_specs=(rows, flat, flat, mats, mats, mats, mats, vecs, vecs, vecs, bias, rows),
        out_specs=(rows, rows, mats, mats, mats, mats, vecs, vecs, vecs, bias),
        check_vma=False,
    )
```

```python
import jax
import jax.numpy as jnp
from jax import lax
from jax.experimental import pallas as pl
from jax.experimental.pallas import tpu as pltpu
from jax.sharding import PartitionSpec as P

NORM_EPS = 1e-06
NEG_FILL = -1e30
F32 = jnp.float32
BF16 = jnp.bfloat16
MESH = pl.DeviceIdType.MESH
NT = (((1,), (1,)), ((), ()))
TN = (((0,), (0,)), ((), ()))
NN = (((1,), (0,)), ((), ()))
VMEM_LIMIT = 63 * 1024 * 1024


def dot(left, right, dims=NN):
    return lax.dot_general(left, right, dims, preferred_element_type=F32)


def lanes(start, size=128):
    return pl.ds(pl.multiple_of(start, 128), size)


class Place:
    def __init__(self):
        self.f = lax.axis_index("fsdp")
        self.s = lax.axis_index("seq")
        self.y = self.s // 4
        self.xl = (self.s // 2) % 2
        self.c = self.s % 2
        self.yp = (self.y + 1) % 4
        self.ym = (self.y + 3) % 4
        self.yo = (self.y + 2) % 4
        self.chip = self.s // 2
        self.j = self.y * 2 + self.c
        self.core = (self.f, self.slot(self.y, self.xl, 1 - self.c))
        self.xpart = (self.f, self.slot(self.y, 1 - self.xl, self.c))
        self.up = (self.f, self.slot(self.yp, self.xl, self.c))
        self.down = (self.f, self.slot(self.ym, self.xl, self.c))

    def slot(self, y, xl, c):
        return (y * 2 + xl) * 2 + c


def greet(me):
    barrier = pltpu.get_barrier_semaphore()
    for step in range(1, 8):
        pl.semaphore_signal(
            barrier, inc=1, device_id=((me.f + step) % 8, me.s), device_id_type=MESH
        )
    for step in range(1, 16):
        pl.semaphore_signal(
            barrier, inc=1, device_id=(me.f, (me.s + step) % 16), device_id_type=MESH
        )


def all_met():
    pl.semaphore_wait(pltpu.get_barrier_semaphore(), 22)


class Wire:
    def __init__(self, send_sem, recv_sem):
        self.send_sem, self.recv_sem = send_sem, recv_sem
        self.used = 0
        self.sent = []

    def send(self, src, dst, device):
        k = self.used
        self.used += 1
        copy = pltpu.make_async_remote_copy(
            src_ref=src,
            dst_ref=dst,
            send_sem=self.send_sem.at[k],
            recv_sem=self.recv_sem.at[k],
            device_id=device,
            device_id_type=MESH,
        )
        copy.start()
        self.sent.append(copy)
        return copy

    def drain(self):
        for copy in self.sent:
            copy.wait_send()
        self.sent = []


class Scatter:
    def __init__(self, me, send_sem, recv_sem, out, into):
        self.me, self.out, self.into = me, out, into
        self.send_sem, self.recv_sem = send_sem, recv_sem

    def copy(self, k, e, peer, arriving):
        return pltpu.make_async_remote_copy(
            src_ref=self.out.at[peer],
            dst_ref=self.into.at[peer if arriving else self.me.s],
            send_sem=self.send_sem.at[2 * k + e],
            recv_sem=self.recv_sem.at[2 * k + (e if arriving else self.me.c)],
            device_id=(self.me.f, peer),
            device_id_type=MESH,
        )

    def send(self, k):
        chip = (self.me.chip + 1 + k) % 8
        self.copy(k, 0, chip * 2, False).start()
        self.copy(k, 1, chip * 2 + 1, False).start()

    def keep(self, wire):
        me = self.me
        self.into[me.s] = self.out[me.s]
        other = me.s + 1 - 2 * me.c
        self.partner = wire.send(self.out.at[other], self.into.at[me.s], me.core)

    def finish(self):
        def collect(k, carry):
            there, back = (self.me.chip + 1 + k) % 8, (self.me.chip + 7 - k) % 8
            for e in range(2):
                self.copy(k, e, there * 2 + e, False).wait_send()
                self.copy(k, e, back * 2 + e, True).wait_recv()
            return carry

        lax.fori_loop(0, 7, collect, 0)
        self.partner.wait_recv()


def to_fsdp(wire, me, src_of, dst_of):
    copies = []
    for step in range(1, 8):
        peer = (me.f + step) % 8
        copies.append(wire.send(src_of(peer), dst_of(me.f), (peer, me.s)))
    return copies


def arrived(copies):
    for copy in copies:
        copy.wait_recv()


class Gather8:
    def __init__(self, wire, me, ref):
        self.wire, self.me, self.ref = wire, me, ref
        h = ref.shape[1] // 2
        self.head, self.tail = pl.ds(0, h), pl.ds(h, h)

    def slot(self, y):
        return y * 2 + self.me.c

    def push(self, y, part, device):
        at = self.ref.at[self.slot(y)] if part is None else self.ref.at[self.slot(y), part]
        return self.wire.send(at, at, device)

    def start(self):
        me = self.me
        self.up = [self.push(me.y, self.head, me.up)]
        self.down = [self.push(me.y, self.tail, me.down)]
        self.up.append(self.push(me.y, self.tail, me.up))
        self.down.append(self.push(me.y, self.head, me.down))
        self.cores = [self.push(me.y, None, me.core)]

    def relay(self):
        me = self.me
        self.up[0].wait_recv()
        self.far = [self.push(me.ym, self.head, me.up)]
        self.down[0].wait_recv()
        self.far.append(self.push(me.yp, self.tail, me.down))

    def middle(self):
        me = self.me
        self.up[1].wait_recv()
        self.cores.append(self.push(me.ym, None, me.core))
        self.down[1].wait_recv()
        self.cores.append(self.push(me.yp, None, me.core))

    def last(self):
        arrived(self.far)
        self.cores.append(self.push(self.me.yo, None, self.me.core))

    def finish(self):
        arrived(self.cores)


class Gather16:
    def __init__(self, wire, me, ref):
        self.wire, self.me, self.ref = wire, me, ref
        h = ref.shape[1] // 2
        self.head, self.tail = pl.ds(0, h), pl.ds(h, h)
        self.cores = []

    def slot(self, y, other):
        me = self.me
        return me.slot(y, 1 - me.xl if other else me.xl, me.c)

    def push(self, y, other, part, device):
        at = self.slot(y, other)
        at = self.ref.at[at] if part is None else self.ref.at[at, part]
        return self.wire.send(at, at, device)

    def to_core(self, y, other):
        self.cores.append((self.push(y, other, None, self.me.core), y, other))

    def spread(self, other):
        me = self.me
        up = [self.push(me.y, other, self.head, me.up)]
        down = [self.push(me.y, other, self.tail, me.down)]
        up.append(self.push(me.y, other, self.tail, me.up))
        down.append(self.push(me.y, other, self.head, me.down))
        return up, down

    def start(self):
        me = self.me
        self.cross = [self.push(me.y, False, part, me.xpart) for part in (self.head, self.tail)]
        self.near = [self.spread(False)]
        self.to_core(me.y, False)

    def relay(self, other):
        me = self.me
        up, down = self.near[int(other)]
        up[0].wait_recv()
        far = [self.push(me.ym, other, self.head, me.up)]
        down[0].wait_recv()
        far.append(self.push(me.yp, other, self.tail, me.down))
        return far

    def middle(self, other):
        up, down = self.near[int(other)]
        up[1].wait_recv()
        self.to_core(self.me.ym, other)
        down[1].wait_recv()
        self.to_core(self.me.yp, other)

    def run(self, use=lambda slot: None):
        me = self.me
        far_own = self.relay(False)
        arrived(self.cross)
        self.near.append(self.spread(True))
        self.to_core(me.y, True)
        use(self.slot(me.y, False))
        use(self.slot(me.y, True))
        self.middle(False)
        far_part = self.relay(True)
        use(self.slot(me.ym, False))
        use(self.slot(me.yp, False))
        arrived(far_own)
        self.to_core(me.yo, False)
        use(self.slot(me.yo, False))
        self.middle(True)
        use(self.slot(me.ym, True))
        use(self.slot(me.yp, True))
        for copy, y, other in self.cores[:4]:
            copy.wait_recv()
            use(me.slot(y, 1 - me.xl if other else me.xl, 1 - me.c))
        arrived(far_part)
        self.to_core(me.yo, True)
        use(self.slot(me.yo, True))
        for copy, y, other in self.cores[4:]:
            copy.wait_recv()
            use(me.slot(y, 1 - me.xl if other else me.xl, 1 - me.c))


class Reduce8:
    def __init__(self, wire, me, part, from_core, from_far, from_near):
        self.wire, self.me, self.part = wire, me, part
        self.from_core, self.from_far, self.from_near = from_core, from_far, from_near
        self.order = (me.yo, me.yp, me.ym, me.y)

    def start(self):
        me = self.me
        self.cores = []
        for d, y in enumerate(self.order):
            src = self.part.at[y * 2 + 1 - me.c]
            self.cores.append(self.wire.send(src, self.from_core.at[d], me.core))

    def combine(self, d):
        self.cores[d].wait_recv()
        own = self.part[self.order[d] * 2 + self.me.c]
        total = own.astype(F32) + self.from_core[d].astype(F32)
        self.from_core[d] = total.astype(BF16)

    def far(self):
        w, me, acc = self.wire, self.me, self.from_core
        h = acc.shape[1] // 2
        self.head, self.tail = pl.ds(0, h), pl.ds(h, h)
        self.combine(0)
        self.f_up = w.send(acc.at[0, self.head], self.from_far.at[0], me.up)
        self.f_down = w.send(acc.at[0, self.tail], self.from_far.at[1], me.down)
        self.combine(1)
        self.n_up = [w.send(acc.at[1, self.tail], self.from_near.at[0, self.tail], me.up)]
        self.combine(2)
        self.n_down = [w.send(acc.at[2, self.head], self.from_near.at[1, self.head], me.down)]

    def near(self):
        w, me, acc = self.wire, self.me, self.from_core
        self.f_up.wait_recv()
        total = acc[1, self.head].astype(F32) + self.from_far[0].astype(F32)
        acc[1, self.head] = total.astype(BF16)
        self.n_up.append(w.send(acc.at[1, self.head], self.from_near.at[0, self.head], me.up))
        self.f_down.wait_recv()
        total = acc[2, self.tail].astype(F32) + self.from_far[1].astype(F32)
        acc[2, self.tail] = total.astype(BF16)
        self.n_down.append(w.send(acc.at[2, self.tail], self.from_near.at[1, self.tail], me.down))

    def result(self):
        self.cores[3].wait_recv()
        own = self.part[self.me.y * 2 + self.me.c]
        total = own.astype(F32) + self.from_core[3].astype(F32)
        arrived(self.n_up)
        arrived(self.n_down)
        return total + self.from_near[0].astype(F32) + self.from_near[1].astype(F32)


def full_row(pv_all, row):
    return jnp.concatenate(
        [pv_all[f].astype(F32)[row : row + 1, :] for f in range(8)], axis=1
    )


def columns(pv_all, f):
    tile = jnp.concatenate([pv_all[f].astype(F32), jnp.zeros((112, 128), F32)], axis=0)
    return tile.T


def norm_stats(values):
    mean_val = jnp.mean(values, axis=-1, keepdims=True)
    centered = values - mean_val
    variance = jnp.mean(centered * centered, axis=-1, keepdims=True)
    inverse = lax.rsqrt(variance + NORM_EPS)
    return centered * inverse, inverse


def norm_back(cotangent, gain, normed, inverse):
    scaled = cotangent * gain
    first = jnp.mean(scaled, axis=-1, keepdims=True)
    second = jnp.mean(scaled * normed, axis=-1, keepdims=True)
    return inverse * (scaled - first - normed * second)


def column_sum(values):
    return jnp.sum(values, axis=0, keepdims=True)


def half_of(which, pair):
    return jnp.where(which == 0, pair[:, :64], pair[:, 64:])


def beside(which, half):
    zero = jnp.zeros_like(half)
    return jnp.where(
        which == 0,
        jnp.concatenate([half, zero], axis=1),
        jnp.concatenate([zero, half], axis=1),
    )


def fold(piece):
    return jnp.concatenate([piece[:64], piece[64:]], axis=1)


def unfold(packed):
    return jnp.concatenate([packed[:, :64], packed[:, 64:]], axis=0)


def three_parts(values):
    first = values.astype(BF16)
    rest = values - first.astype(F32)
    second = rest.astype(BF16)
    third = (rest - second.astype(F32)).astype(BF16)
    return first.astype(F32), second.astype(F32), third.astype(F32)


def eight(ref):
    total = ref[0].astype(F32)
    for f in range(1, 8):
        total = total + ref[f].astype(F32)
    return total


def layer(
    tok, gout, valid, w_qkv, w_proj, w_fc1, w_fc2, gain_in, shift_in, scale_in, bias_in,
    res, gtok, o_qkv, o_proj, o_fc1, w2_all, o_vec,
    nrm, grd, pv_all, v_all, wq_one, wq_all, wq_use, wp_all, w1_one, w1_all, wqf,
    qa, ka, va, ow, om, at,
    nmg, act, gpre, gn, mp, r_core, r_far, r_near, msg, gat, mid, gmid, atg, gac, gh,
    dw1, dw2, vec, db1,
    ga, qb, kt, dk, dv, dq, qm, qin, kvm, kvin, m_core, m_far, m_near,
    dwp, r1, r2, rp, x1, x2, xp, gp, dwq, rq, gq, vs, vr, vq,
    ss, rs, as_, ar_, bs, br,
):
    me = Place()
    wire = Wire(ss, rs)
    greet(me)
    vin = jnp.broadcast_to(valid[...].astype(F32), (16, 128)).astype(BF16)
    v_all[me.s] = vin
    bias = half_of(me.c, bias_in[:, lanes(me.y * 128)].astype(F32))
    pv_all[me.f] = jnp.concatenate(
        [
            gain_in[...].astype(F32),
            shift_in[...].astype(F32),
            scale_in[...].astype(F32),
            jnp.concatenate([bias, jnp.zeros((1, 64), F32)], axis=1),
            jnp.zeros((5, 128), F32),
        ],
        axis=0,
    ).astype(BF16)
    normed, _ = norm_stats(tok[...].astype(F32))
    nrm[me.s] = normed.astype(BF16)
    parts = [half_of(me.c, w_qkv[:, lanes(p * 1024 + me.chip * 128)]) for p in range(3)]
    wq_one[...] = jnp.concatenate([*parts, jnp.zeros((128, 64), BF16)], axis=1)
    wq_all[me.f] = wq_one[...]
    for f in range(0, 8, 2):
        pair = [half_of(me.c, w_fc1[:, lanes(g * 512 + me.y * 128)]) for g in (f, f + 1)]
        w1_one[:, f * 64 : (f + 2) * 64] = jnp.concatenate(pair, axis=1)
    w1_all[me.f] = w1_one[...]
    wp_all[me.f] = w_proj[...]
    wqf[me.f] = w_qkv[...]
    mine = pl.ds(pl.multiple_of(me.j * 64, 64), 64)
    w2_all[me.f] = w_fc2[mine]
    all_met()

    gather = Gather16(wire, me, nrm)
    gather.start()
    own_pv = pv_all.at[me.f]
    got_pv = to_fsdp(wire, me, lambda p: own_pv, lambda f: pv_all.at[f])
    got_wq = to_fsdp(wire, me, lambda p: wq_one, lambda f: wq_all.at[f])
    got_v = []
    for step in range(1, 16):
        peer = (me.s + step) % 16
        got_v.append(wire.send(v_all.at[me.s], v_all.at[me.s], (me.f, peer)))
    half = pl.ds(pl.multiple_of(me.c * 64, 64), 64)

    far_own = None
    ready = {}

    def prepare():
        arrived(got_pv)
        arrived(got_wq)
        shifts = jnp.zeros((1, 256), F32)
        for f in range(8):
            cols = columns(pv_all, f)
            weight = wq_all[f]
            wq_use[f * 128 : (f + 1) * 128, :] = (weight.astype(F32) * cols[:, 0:1]).astype(BF16)
            row = jnp.broadcast_to(pv_all[f].astype(F32)[2:3, :], (16, 128)).astype(BF16)
            shifts = shifts + dot(row, weight)[0:1]
        own = half_of(me.c, pv_all[me.chip].astype(F32))
        zero = jnp.zeros((1, 64), F32)
        ready["bias"] = shifts + jnp.concatenate([own[4:5], zero, own[5:6], zero], axis=1)
        ready["wp"] = to_fsdp(
            wire, me, lambda p: w_proj.at[half], lambda f: wp_all.at[f, half]
        )
        ready["w1"] = to_fsdp(wire, me, lambda p: w1_one, lambda f: w1_all.at[f])
        arrived(got_v)
        flags = v_all[:, 0, :].astype(F32)
        flags = jnp.concatenate([flags, jnp.zeros((112, 128), F32)], axis=0).T
        lane = lax.broadcasted_iota(jnp.int32, (128, 64), 1)
        for blk in range(16):
            mask = (1.0 - flags[:, blk : blk + 1]) * NEG_FILL
            ext = jnp.where(lane == 0, mask, jnp.where(lane < 4, 1.0, 0.0))
            ka[blk * 128 : (blk + 1) * 128, 64:] = ext.astype(BF16)

    ext_lane = lax.broadcasted_iota(jnp.int32, (128, 64), 1)
    q_ext = jnp.where(ext_lane == 0, 1.0, 0.0).astype(BF16)
    v_ext = jnp.where(ext_lane < 3, 1.0, 0.0).astype(BF16)

    def project(slot):
        if not ready:
            prepare()
        qkv = dot(nrm[slot], wq_use[...]) + ready["bias"]
        rows = pl.ds(pl.multiple_of(slot * 128, 128), 128)
        query = (qkv[:, :64].astype(BF16) * 0.125).astype(BF16)
        qa[rows, :] = jnp.concatenate([query, q_ext], axis=1)
        ka[rows, :64] = qkv[:, 64:128].astype(BF16)
        va[rows, :] = jnp.concatenate([qkv[:, 128:192].astype(BF16), v_ext], axis=1)

    gather.run(project)
    grd[me.j] = (full_row(pv_all, 9) * gout[...].astype(F32)).astype(BF16)
    grad_gather = Gather8(wire, me, grd)
    grad_gather.start()
    got_w2 = to_fsdp(wire, me, lambda p: w_fc2.at[mine], lambda f: w2_all.at[f])

    heads_out = Scatter(me, as_, ar_, om, at)
    out_lane = lax.broadcasted_iota(jnp.int32, (256, 128), 1)

    def attend(k):
        chip = (me.chip + 1 + k) % 8
        rows = pl.ds(pl.multiple_of(chip * 256, 256), 256)
        scores = dot(qa[rows, :], ka[...], NT)
        row_max = jnp.max(scores, axis=1, keepdims=True)
        terms = jnp.exp(scores - row_max).astype(BF16)
        mixed = dot(terms, va[...])
        total = mixed[:, 64:65]
        heads = mixed / total
        log_sum = row_max + jnp.log(total)
        ow[rows, :] = jnp.where(out_lane < 64, heads, log_sum)
        rounded = heads[:, :64].astype(BF16)
        for e in range(2):
            om[chip * 2 + e] = fold(rounded[e * 128 : (e + 1) * 128])

    def attend_send(k, carry):
        attend(k)
        heads_out.send(k)
        return carry

    lax.fori_loop(0, 2, attend_send, 0)
    grad_gather.relay()
    lax.fori_loop(2, 5, attend_send, 0)
    grad_gather.middle()
    lax.fori_loop(5, 7, attend_send, 0)
    grad_gather.last()
    arrived(ready["wp"])
    swap = [wire.send(wp_all.at[f, half], wp_all.at[f, half], me.core) for f in range(8)]
    attend(7)
    heads_out.keep(wire)
    heads_out.finish()

    attn_tok = jnp.concatenate([unfold(at[h]) for h in range(16)], axis=1)
    atg[me.j] = attn_tok
    arrived(swap)
    scale_one = full_row(pv_all, 8)
    branch = dot(attn_tok, wp_all[...].reshape(1024, 1024)) + full_row(pv_all, 6)
    middle = tok[...].astype(F32) + scale_one * branch
    mid[...] = middle
    normed, inverse = norm_stats(middle)
    gain = full_row(pv_all, 1)
    nmg[me.j] = (normed * gain + full_row(pv_all, 3)).astype(BF16)
    gather = Gather8(wire, me, nmg)
    gather.start()
    attn_gather = Gather8(wire, me, atg)
    grad_gather.finish()
    gather.relay()
    gather.middle()
    attn_gather.start()
    gather.last()
    arrived(ready["w1"])
    arrived(got_w2)
    got_wqf = to_fsdp(wire, me, lambda p: w_qkv.at[half], lambda f: wqf.at[f, half])
    bias_one = jnp.concatenate(
        [pv_all[f].astype(F32)[10:11, :64] for f in range(8)], axis=1
    )
    gather.finish()

    def feed(b, carry):
        two = pl.ds(2 * b, 2)
        rows = pl.ds(pl.multiple_of(b * 256, 256), 256)
        w1 = w1_all[...].reshape(1024, 512)
        w2 = w2_all[...].reshape(512, 1024)
        pre = dot(nmg[two].reshape(256, 1024), w1) + bias_one
        cdf = 0.5 * (1.0 + lax.erf(pre * 0.7071067811865476))
        acts = (pre * cdf).astype(BF16)
        act[rows, :] = acts
        mp[two] = dot(acts, w2).astype(BF16).reshape(2, 128, 1024)
        grad_act = dot(grd[two].reshape(256, 1024), w2, NT)
        slope = cdf + pre * jnp.exp(-0.5 * pre * pre) * 0.3989422804014327
        grad_pre = (grad_act * slope).astype(BF16)
        gpre[rows, :] = grad_pre
        gn[two] = dot(grad_pre, w1, NT).astype(BF16).reshape(2, 128, 1024)
        return carry + column_sum(grad_pre.astype(F32))

    db1[...] = lax.fori_loop(0, 4, feed, jnp.zeros((1, 512), F32))
    reduce = Reduce8(wire, me, gn, r_core, r_far, r_near)
    reduce.start()
    reduce.far()
    attn_gather.relay()
    dw2[...] = dot(act[...], grd[...].reshape(1024, 1024), TN).astype(BF16).reshape(8, 64, 1024)
    reduce.near()
    got = to_fsdp(wire, me, lambda p: dw2.at[p], lambda f: r2.at[f])
    dw1[...] = dot(nmg[...].reshape(1024, 1024), gpre[...], TN).astype(BF16).reshape(8, 128, 512)
    got += to_fsdp(wire, me, lambda p: dw1.at[p], lambda f: r1.at[f])
    r1[me.f] = dw1[me.f]
    r2[me.f] = dw2[me.f]
    cotangent = reduce.result()
    grad_middle = gout[...].astype(F32) + norm_back(cotangent, gain, normed, inverse)
    gmid[...] = grad_middle
    grad_attn = (scale_one * grad_middle).astype(BF16)
    gat[...] = grad_attn
    grad_tok = dot(grad_attn, wp_all[...].reshape(1024, 1024), NT).astype(BF16)
    for h in range(16):
        msg[h] = fold(grad_tok[:, h * 64 : (h + 1) * 64])
    gh[me.s] = msg[me.s]
    got_gh = []
    for step in range(1, 16):
        peer = (me.s + step) % 16
        got_gh.append(wire.send(msg.at[peer], gh.at[me.s], (me.f, peer)))
    got_gac = []
    for step in range(1, 8):
        peer = (me.j + step) % 8
        device = (me.f, me.slot(peer // 2, me.xl, peer % 2))
        got_gac.append(wire.send(gat.at[:, lanes(peer * 128)], gac.at[me.j], device))
    gac[me.j] = gat[:, lanes(me.j * 128)]
    mlp = Reduce8(wire, me, mp, m_core, m_far, m_near)
    mlp.start()
    zero = jnp.zeros((1, 1024), F32)
    vec[...] = jnp.concatenate(
        [
            zero,
            column_sum(cotangent * normed),
            zero,
            column_sum(cotangent),
            zero,
            zero,
            column_sum(grad_attn.astype(F32)),
            column_sum(grd[me.j].astype(F32)),
            column_sum(grad_middle * branch),
            jnp.zeros((7, 1024), F32),
        ],
        axis=0,
    )
    attn_gather.middle()
    attn_gather.last()
    mlp.far()
    lane = lax.broadcasted_iota(jnp.int32, (128, 128), 1)
    for blk in range(16):
        rows = slice(blk * 128, (blk + 1) * 128)
        l1, l2, l3 = three_parts(-ow[rows, 64:65])
        wide = qa[rows, :].astype(F32)
        wide = jnp.where(lane == 65, l1, wide)
        wide = jnp.where(lane == 66, l2, wide)
        wide = jnp.where(lane == 67, l3, wide)
        qb[rows, :] = wide.astype(BF16)
        kt[:, rows] = ka[rows, :].astype(F32).T.astype(BF16)
    dk[...] = jnp.zeros_like(dk)
    dv[...] = jnp.zeros_like(dv)

    arrived(got_gh)
    for blk in range(16):
        rows = slice(blk * 128, (blk + 1) * 128)
        grad = unfold(gh[blk])
        delta = jnp.sum(grad.astype(F32) * ow[rows, :64], axis=1, keepdims=True)
        d1, d2, d3 = three_parts(-delta)
        wide = jnp.concatenate([grad, jnp.zeros((128, 64), BF16)], axis=1).astype(F32)
        wide = jnp.where(lane == 64, d1, wide)
        wide = jnp.where(lane == 65, d2, wide)
        wide = jnp.where(lane == 66, d3, wide)
        ga[rows, :] = wide.astype(BF16)

    queries_out = Scatter(me, bs, br, qm, qin)

    def back(k):
        chip = (me.chip + 1 + k) % 8
        rows = pl.ds(pl.multiple_of(chip * 256, 256), 256)
        query, grad = qb[rows, :], ga[rows, :]
        probs = jnp.exp(dot(ka[...], query, NT))
        dv[...] += dot(probs.astype(BF16), grad)
        slope = dot(va[...], grad, NT)
        scores = (probs * slope).astype(BF16)
        dk[...] += dot(scores, query)
        turned = dot(kt[...], scores)
        grad_query = (turned.T[:, :64] * 0.125).astype(BF16)
        dq[rows, :64] = grad_query
        for e in range(2):
            qm[chip * 2 + e] = fold(grad_query[e * 128 : (e + 1) * 128])

    def back_send(k, carry):
        back(k)
        queries_out.send(k)
        return carry

    lax.fori_loop(0, 3, back_send, 0)
    mlp.near()
    arrived(got_gac)
    attn_gather.finish()
    for f in range(8):
        tok_cols = atg[:, :, f * 128 : (f + 1) * 128].reshape(1024, 128)
        dwp[f] = dot(tok_cols, gac[...].reshape(1024, 128), TN).astype(BF16)
    got += to_fsdp(wire, me, lambda p: dwp.at[p], lambda f: rp.at[f])
    rp[me.f] = dwp[me.f]
    arrived(got_wqf)
    swap = [wire.send(wqf.at[f, half], wqf.at[f, half], me.core) for f in range(8)]
    lax.fori_loop(3, 6, back_send, 0)
    arrived(got)
    x1[0] = eight(r1).astype(BF16)
    x2[0] = eight(r2).astype(BF16)
    xp[0] = eight(rp).astype(BF16)
    crossed = [wire.send(x.at[0], x.at[1], me.xpart) for x in (x1, x2, xp)]
    lax.fori_loop(6, 7, back_send, 0)
    back(7)
    queries_out.keep(wire)

    for blk in range(16):
        rows = slice(blk * 128, (blk + 1) * 128)
        grad_key, grad_value = dk[rows, :64].astype(BF16), dv[rows, :64].astype(BF16)
        kvm[blk] = jnp.concatenate([grad_key, grad_value], axis=1)
        dq[rows, 64:128] = grad_key
        dq[rows, 128:] = jnp.concatenate([grad_value, jnp.zeros((128, 64), BF16)], axis=1)
    got_kv = []
    for step in range(1, 16):
        peer = (me.s + step) % 16
        got_kv.append(wire.send(kvm.at[peer], kvin.at[me.s], (me.f, peer)))
    kvin[me.s] = kvm[me.s]

    mlp_out = mlp.result() + full_row(pv_all, 7)
    res[...] = (mid[...] + full_row(pv_all, 9) * mlp_out).astype(BF16)
    vec[9:10, :] = column_sum(gout[...].astype(F32) * mlp_out)
    sums = column_sum(dq[...].astype(F32))
    got_q, got_vec = [], []
    for step in range(1, 9):
        f = (me.f + step) % 8
        cols = columns(pv_all, f)
        product = dot(nrm[:, :, lanes(f * 128)].reshape(2048, 128), dq[...], TN)
        grad_wq = product * cols[:, 0:1] + cols[:, 2:3] * sums
        weight = wq_all[f].astype(F32)
        first = jnp.sum(weight * product, axis=1, keepdims=True)
        second = jnp.sum(weight * sums, axis=1, keepdims=True)
        turned = jnp.where(lane == 0, first, jnp.where(lane == 1, second, 0.0)).T
        rows = vec[:, lanes(f * 128)]
        piece = half_of(f % 2, db1[:, lanes((f // 2) * 128)])
        bias = beside(me.c, piece)
        here = me.chip == f
        packed = jnp.concatenate(
            [
                turned[0:1],
                rows[1:2],
                turned[1:2],
                rows[3:4],
                jnp.where(here, beside(me.c, sums[:, :64]), 0.0),
                jnp.where(here, beside(me.c, sums[:, 128:192]), 0.0),
                rows[6:10],
                *[jnp.where(me.y == y, bias, 0.0) for y in range(4)],
                jnp.zeros((2, 128), F32),
            ],
            axis=0,
        )
        if step < 8:
            dwq[f] = grad_wq.astype(BF16)
            vs[f] = packed
            got_q.append(wire.send(dwq.at[f], rq.at[me.f], (f, me.s)))
            got_vec.append(wire.send(vs.at[f], vr.at[me.f], (f, me.s)))
        else:
            rq[me.f] = grad_wq.astype(BF16)
            vr[me.f] = packed

    arrived(crossed)
    gathers = []
    for x, g in ((x1, w1_all), (x2, w2_all), (xp, gp)):
        g[me.j] = (x[0].astype(F32) + x[1].astype(F32)).astype(BF16)
        gathers.append(Gather8(wire, me, g))
    for gather in gathers:
        gather.start()

    queries_out.finish()
    arrived(got_kv)
    arrived(swap)
    parts = [unfold(qin[h]) for h in range(16)]
    parts += [kvin[h][:, :64] for h in range(16)] + [kvin[h][:, 64:] for h in range(16)]
    grad_qkv = jnp.concatenate(parts, axis=1)
    cotangent = dot(grad_qkv, wqf[...].reshape(1024, 3072), NT)

    arrived(got_q)
    gq[me.s] = eight(rq).astype(BF16)
    gather_q = Gather16(wire, me, gq)
    gather_q.start()
    arrived(got_vec)
    vq[me.s] = eight(vr)
    got_vq = []
    for step in range(1, 16):
        peer = (me.s + step) % 16
        got_vq.append(wire.send(vq.at[me.s], vq.at[me.s], (me.f, peer)))
    for gather in gathers:
        gather.relay()
    for gather in gathers:
        gather.middle()
    normed, inverse = norm_stats(tok[...].astype(F32))
    gtok[...] = gmid[...] + norm_back(cotangent, full_row(pv_all, 0), normed, inverse)
    for gather in gathers:
        gather.last()
    gather_q.run()
    for part in range(3):
        cols = slice(part * 64, (part + 1) * 64)
        for k in range(8):
            pair = jnp.concatenate([gq[2 * k, :, cols], gq[2 * k + 1, :, cols]], axis=1)
            o_qkv[:, part * 1024 + k * 128 : part * 1024 + (k + 1) * 128] = pair
    for gather in gathers:
        gather.finish()
    for j in range(8):
        o_proj[:, j * 128 : (j + 1) * 128] = gp[j]
    for f in range(8):
        cols = slice(f * 64, (f + 1) * 64)
        for k in range(4):
            pair = jnp.concatenate([w1_all[2 * k, :, cols], w1_all[2 * k + 1, :, cols]], axis=1)
            o_fc1[:, f * 512 + k * 128 : f * 512 + (k + 1) * 128] = pair
    arrived(got_vq)
    total = vq[0]
    for s in range(1, 16):
        total = total + vq[s]
    o_vec[...] = total
    wire.drain()


OUTS = (
    ((128, 1024), BF16),
    ((128, 1024), F32),
    ((128, 3072), BF16),
    ((128, 1024), BF16),
    ((128, 4096), BF16),
    ((8, 64, 1024), BF16),
    ((16, 128), F32),
)
SCRATCH = (
    ((16, 128, 1024), BF16),
    ((8, 128, 1024), BF16),
    ((8, 16, 128), BF16),
    ((16, 16, 128), BF16),
    ((128, 256), BF16),
    ((8, 128, 256), BF16),
    ((1024, 256), BF16),
    ((8, 128, 1024), BF16),
    ((128, 512), BF16),
    ((8, 128, 512), BF16),
    ((8, 128, 3072), BF16),
    ((2048, 128), BF16),
    ((2048, 128), BF16),
    ((2048, 128), BF16),
    ((2048, 128), F32),
    ((16, 64, 128), BF16),
    ((16, 64, 128), BF16),
    ((8, 128, 1024), BF16),
    ((1024, 512), BF16),
    ((1024, 512), BF16),
    ((8, 128, 1024), BF16),
    ((8, 128, 1024), BF16),
    ((4, 128, 1024), BF16),
    ((2, 64, 1024), BF16),
    ((2, 128, 1024), BF16),
    ((16, 64, 128), BF16),
    ((128, 1024), BF16),
    ((128, 1024), F32),
    ((128, 1024), F32),
    ((8, 128, 1024), BF16),
    ((8, 128, 128), BF16),
    ((16, 64, 128), BF16),
    ((8, 128, 512), BF16),
    ((8, 64, 1024), BF16),
    ((16, 1024), F32),
    ((1, 512), F32),
    ((2048, 128), BF16),
    ((2048, 128), BF16),
    ((128, 2048), BF16),
    ((2048, 128), F32),
    ((2048, 128), F32),
    ((2048, 256), BF16),
    ((16, 64, 128), BF16),
    ((16, 64, 128), BF16),
    ((16, 128, 128), BF16),
    ((16, 128, 128), BF16),
    ((4, 128, 1024), BF16),
    ((2, 64, 1024), BF16),
    ((2, 128, 1024), BF16),
    ((8, 128, 128), BF16),
    ((8, 128, 512), BF16),
    ((8, 64, 1024), BF16),
    ((8, 128, 128), BF16),
    ((2, 128, 512), BF16),
    ((2, 64, 1024), BF16),
    ((2, 128, 128), BF16),
    ((8, 128, 128), BF16),
    ((8, 128, 256), BF16),
    ((8, 128, 256), BF16),
    ((16, 128, 256), BF16),
    ((8, 16, 128), F32),
    ((8, 16, 128), F32),
    ((16, 16, 128), F32),
)
COPIES = 352


def body(
    tokens, image_ids, valid, w_qkv, w_proj, w_fc1, w_fc2,
    norm_gain, shifts, layer_scale, fc1_bias, grad_out,
):
    semaphores = [pltpu.SemaphoreType.DMA((n,)) for n in (COPIES, COPIES, 14, 14, 14, 14)]
    whole = pl.BlockSpec(memory_space=pltpu.VMEM)
    res, gtok, g_qkv, g_proj, g_fc1, g_fc2, g_vec = pl.pallas_call(
        layer,
        out_shape=[jax.ShapeDtypeStruct(shape, dtype) for shape, dtype in OUTS],
        in_specs=[whole] * 11,
        out_specs=[whole] * len(OUTS),
        scratch_shapes=[pltpu.VMEM(shape, dtype) for shape, dtype in SCRATCH] + semaphores,
        name="layer",
        compiler_params=pltpu.CompilerParams(
            collective_id=1, has_side_effects=True, vmem_limit_bytes=VMEM_LIMIT
        ),
    )(
        tokens, grad_out, valid.reshape(1, 128), w_qkv[0], w_proj[0], w_fc1[0], w_fc2[0],
        norm_gain[0], shifts[0], layer_scale[0], fc1_bias,
    )
    return (
        res,
        gtok,
        g_qkv[None].astype(F32),
        g_proj[None].astype(F32),
        g_fc1[None].astype(F32),
        g_fc2.reshape(1, 512, 1024).astype(F32),
        g_vec[None, 0:2],
        g_vec[None, 2:8],
        g_vec[None, 8:10],
        g_vec[10:14].reshape(1, 512),
    )


def solution(mesh):
    rows = P(("fsdp", "seq"), None)
    flat = P(("fsdp", "seq"))
    mats = P(None, "fsdp", None)
    vecs = P(None, None, "fsdp")
    bias = P(None, "fsdp")
    return jax.shard_map(
        body,
        mesh=mesh,
        in_specs=(rows, flat, flat, mats, mats, mats, mats, vecs, vecs, vecs, bias, rows),
        out_specs=(rows, rows, mats, mats, mats, mats, vecs, vecs, vecs, bias),
        check_vma=False,
    )
```

```python
import jax
import jax.numpy as jnp
from jax import lax
from jax.experimental import pallas as pl
from jax.experimental.pallas import tpu as pltpu
from jax.sharding import PartitionSpec as P

NORM_EPS = 1e-06
NEG_FILL = -1e30
F32 = jnp.float32
BF16 = jnp.bfloat16
MESH = pl.DeviceIdType.MESH
NT = (((1,), (1,)), ((), ()))
TN = (((0,), (0,)), ((), ()))
NN = (((1,), (0,)), ((), ()))
VMEM_LIMIT = 63 * 1024 * 1024


def dot(left, right, dims=NN):
    return lax.dot_general(left, right, dims, preferred_element_type=F32)


def lanes(start, size=128):
    return pl.ds(pl.multiple_of(start, 128), size)


class Place:
    def __init__(self):
        self.f = lax.axis_index("fsdp")
        self.s = lax.axis_index("seq")
        self.y = self.s // 4
        self.xl = (self.s // 2) % 2
        self.c = self.s % 2
        self.yp = (self.y + 1) % 4
        self.ym = (self.y + 3) % 4
        self.yo = (self.y + 2) % 4
        self.chip = self.s // 2
        self.j = self.y * 2 + self.c
        self.core = (self.f, self.slot(self.y, self.xl, 1 - self.c))
        self.xpart = (self.f, self.slot(self.y, 1 - self.xl, self.c))
        self.up = (self.f, self.slot(self.yp, self.xl, self.c))
        self.down = (self.f, self.slot(self.ym, self.xl, self.c))

    def slot(self, y, xl, c):
        return (y * 2 + xl) * 2 + c


def greet(me):
    barrier = pltpu.get_barrier_semaphore()
    for step in range(1, 8):
        pl.semaphore_signal(
            barrier, inc=1, device_id=((me.f + step) % 8, me.s), device_id_type=MESH
        )
    for step in range(1, 16):
        pl.semaphore_signal(
            barrier, inc=1, device_id=(me.f, (me.s + step) % 16), device_id_type=MESH
        )


def all_met():
    pl.semaphore_wait(pltpu.get_barrier_semaphore(), 22)


class Wire:
    def __init__(self, send_sem, recv_sem):
        self.send_sem, self.recv_sem = send_sem, recv_sem
        self.used = 0
        self.sent = []

    def send(self, src, dst, device):
        k = self.used
        self.used += 1
        copy = pltpu.make_async_remote_copy(
            src_ref=src,
            dst_ref=dst,
            send_sem=self.send_sem.at[k],
            recv_sem=self.recv_sem.at[k],
            device_id=device,
            device_id_type=MESH,
        )
        copy.start()
        self.sent.append(copy)
        return copy

    def settle(self, copies):
        for copy in copies:
            copy.wait_send()
        done = {id(copy) for copy in copies}
        self.sent = [copy for copy in self.sent if id(copy) not in done]

    def drain(self):
        self.settle(list(self.sent))


class Scatter:
    def __init__(self, me, send_sem, recv_sem, out, into):
        self.me, self.out, self.into = me, out, into
        self.send_sem, self.recv_sem = send_sem, recv_sem

    def copy(self, k, e, peer, arriving):
        return pltpu.make_async_remote_copy(
            src_ref=self.out.at[peer],
            dst_ref=self.into.at[peer if arriving else self.me.s],
            send_sem=self.send_sem.at[2 * k + e],
            recv_sem=self.recv_sem.at[2 * k + (e if arriving else self.me.c)],
            device_id=(self.me.f, peer),
            device_id_type=MESH,
        )

    def send(self, k):
        chip = (self.me.chip + 1 + k) % 8
        self.copy(k, 0, chip * 2, False).start()
        self.copy(k, 1, chip * 2 + 1, False).start()

    def keep(self, wire):
        me = self.me
        self.into[me.s] = self.out[me.s]
        other = me.s + 1 - 2 * me.c
        self.partner = wire.send(self.out.at[other], self.into.at[me.s], me.core)

    def finish(self):
        def collect(k, carry):
            there, back = (self.me.chip + 1 + k) % 8, (self.me.chip + 7 - k) % 8
            for e in range(2):
                self.copy(k, e, there * 2 + e, False).wait_send()
                self.copy(k, e, back * 2 + e, True).wait_recv()
            return carry

        lax.fori_loop(0, 7, collect, 0)
        self.partner.wait_recv()


def to_fsdp(wire, me, src_of, dst_of):
    copies = []
    for step in range(1, 8):
        peer = (me.f + step) % 8
        copies.append(wire.send(src_of(peer), dst_of(me.f), (peer, me.s)))
    return copies


def arrived(copies):
    for copy in copies:
        copy.wait_recv()


class Fan:
    def __init__(self, wire, me, src, dst):
        self.wire, self.me, self.src, self.dst = wire, me, src, dst

    def at(self, dz, other=False):
        z, xh = self.me.f // 2, self.me.f % 2
        return ((z + dz) % 4) * 2 + (1 - xh if other else xh)

    def push(self, src, dst, f):
        return self.wire.send(src, dst, (f, self.me.s))

    def start(self):
        slot = self.dst(self.me.f)
        self.cross = self.push(self.src, slot, self.at(0, True))
        self.near = [self.push(self.src, slot, self.at(dz)) for dz in (1, 3)]
        self.far = self.push(self.src, slot, self.at(2))

    def relay_near(self):
        self.cross.wait_recv()
        slot = self.dst(self.at(0, True))
        self.near += [self.push(slot, slot, self.at(dz)) for dz in (1, 3)]

    def relay_far(self):
        self.far.wait_recv()
        slot = self.dst(self.at(2))
        self.near.append(self.push(slot, slot, self.at(0, True)))

    def finish(self):
        arrived(self.near)

    def settle(self):
        self.wire.settle([self.cross, self.far, *self.near])


class FanIn(Fan):
    def __init__(self, wire, me, part, into):
        self.wire, self.me, self.part, self.into = wire, me, part, into

    def start(self):
        part, into = self.part, self.into
        self.over = [self.push(part.at[self.at(2, True)], into.at[6], self.at(0, True))]
        for k, dz in enumerate((1, 3)):
            self.over.append(self.push(part.at[self.at(dz, True)], into.at[4 + k], self.at(dz)))
        self.last = []
        for k, dz in enumerate((1, 3)):
            self.last.append(self.push(part.at[self.at(dz)], into.at[1 + k], self.at(dz)))

    def forward(self):
        part, into = self.part, self.into
        arrived(self.over)
        total = into[4].astype(F32) + into[5].astype(F32) + part[self.at(0, True)].astype(F32)
        into[4] = total.astype(BF16)
        self.last.append(self.push(into.at[4], into.at[0], self.at(0, True)))
        total = into[6].astype(F32) + part[self.at(2)].astype(F32)
        into[6] = total.astype(BF16)
        self.last.append(self.push(into.at[6], into.at[3], self.at(2)))

    def result(self):
        arrived(self.last)
        total = self.part[self.me.f].astype(F32)
        for k in range(4):
            total = total + self.into[k].astype(F32)
        return total


class Gather8:
    def __init__(self, wire, me, ref):
        self.wire, self.me, self.ref = wire, me, ref
        h = ref.shape[1] // 2
        self.head, self.tail = pl.ds(0, h), pl.ds(h, h)

    def slot(self, y):
        return y * 2 + self.me.c

    def push(self, y, part, device):
        at = self.ref.at[self.slot(y)] if part is None else self.ref.at[self.slot(y), part]
        return self.wire.send(at, at, device)

    def start(self):
        me = self.me
        self.up = [self.push(me.y, self.head, me.up)]
        self.down = [self.push(me.y, self.tail, me.down)]
        self.up.append(self.push(me.y, self.tail, me.up))
        self.down.append(self.push(me.y, self.head, me.down))
        self.cores = [self.push(me.y, None, me.core)]

    def relay(self):
        me = self.me
        self.up[0].wait_recv()
        self.far = [self.push(me.ym, self.head, me.up)]
        self.down[0].wait_recv()
        self.far.append(self.push(me.yp, self.tail, me.down))

    def middle(self):
        me = self.me
        self.up[1].wait_recv()
        self.cores.append(self.push(me.ym, None, me.core))
        self.down[1].wait_recv()
        self.cores.append(self.push(me.yp, None, me.core))

    def last(self):
        arrived(self.far)
        self.cores.append(self.push(self.me.yo, None, self.me.core))

    def finish(self):
        arrived(self.cores)


class Gather16:
    def __init__(self, wire, me, ref):
        self.wire, self.me, self.ref = wire, me, ref
        h = ref.shape[1] // 2
        self.head, self.tail = pl.ds(0, h), pl.ds(h, h)
        self.cores = []

    def slot(self, y, other):
        me = self.me
        return me.slot(y, 1 - me.xl if other else me.xl, me.c)

    def push(self, y, other, part, device):
        at = self.slot(y, other)
        at = self.ref.at[at] if part is None else self.ref.at[at, part]
        return self.wire.send(at, at, device)

    def to_core(self, y, other):
        self.cores.append((self.push(y, other, None, self.me.core), y, other))

    def spread(self, other):
        me = self.me
        up = [self.push(me.y, other, self.head, me.up)]
        down = [self.push(me.y, other, self.tail, me.down)]
        up.append(self.push(me.y, other, self.tail, me.up))
        down.append(self.push(me.y, other, self.head, me.down))
        return up, down

    def start(self):
        me = self.me
        self.cross = [self.push(me.y, False, part, me.xpart) for part in (self.head, self.tail)]
        self.near = [self.spread(False)]
        self.to_core(me.y, False)

    def relay(self, other):
        me = self.me
        up, down = self.near[int(other)]
        up[0].wait_recv()
        far = [self.push(me.ym, other, self.head, me.up)]
        down[0].wait_recv()
        far.append(self.push(me.yp, other, self.tail, me.down))
        return far

    def middle(self, other):
        up, down = self.near[int(other)]
        up[1].wait_recv()
        self.to_core(self.me.ym, other)
        down[1].wait_recv()
        self.to_core(self.me.yp, other)

    def run(self, crossed=lambda: None, prepare=lambda: None, use=lambda slot: None):
        me = self.me
        far_own = self.relay(False)
        arrived(self.cross)
        self.near.append(self.spread(True))
        self.to_core(me.y, True)
        crossed()
        self.middle(False)
        far_part = self.relay(True)
        arrived(far_own)
        self.to_core(me.yo, False)
        prepare()
        use(self.slot(me.y, False))
        use(self.slot(me.y, True))
        use(self.slot(me.ym, False))
        use(self.slot(me.yp, False))
        self.middle(True)
        use(self.slot(me.yo, False))
        for copy, y, other in self.cores[:3]:
            copy.wait_recv()
            use(me.slot(y, 1 - me.xl if other else me.xl, 1 - me.c))
        arrived(far_part)
        self.to_core(me.yo, True)
        use(self.slot(me.ym, True))
        use(self.slot(me.yp, True))
        use(self.slot(me.yo, True))
        for copy, y, other in self.cores[3:]:
            copy.wait_recv()
            use(me.slot(y, 1 - me.xl if other else me.xl, 1 - me.c))


class Reduce8:
    def __init__(self, wire, me, part, from_core, from_far, from_near):
        self.wire, self.me, self.part = wire, me, part
        self.from_core, self.from_far, self.from_near = from_core, from_far, from_near
        self.order = (me.yo, me.yp, me.ym, me.y)

    def start(self):
        me = self.me
        self.cores = []
        for d, y in enumerate(self.order):
            src = self.part.at[y * 2 + 1 - me.c]
            self.cores.append(self.wire.send(src, self.from_core.at[d], me.core))

    def combine(self, d):
        self.cores[d].wait_recv()
        own = self.part[self.order[d] * 2 + self.me.c]
        total = own.astype(F32) + self.from_core[d].astype(F32)
        self.from_core[d] = total.astype(BF16)

    def far(self):
        w, me, acc = self.wire, self.me, self.from_core
        h = acc.shape[1] // 2
        self.head, self.tail = pl.ds(0, h), pl.ds(h, h)
        self.combine(0)
        self.f_up = w.send(acc.at[0, self.head], self.from_far.at[0], me.up)
        self.f_down = w.send(acc.at[0, self.tail], self.from_far.at[1], me.down)
        self.combine(1)
        self.n_up = [w.send(acc.at[1, self.tail], self.from_near.at[0, self.tail], me.up)]
        self.combine(2)
        self.n_down = [w.send(acc.at[2, self.head], self.from_near.at[1, self.head], me.down)]

    def near(self):
        w, me, acc = self.wire, self.me, self.from_core
        self.f_up.wait_recv()
        total = acc[1, self.head].astype(F32) + self.from_far[0].astype(F32)
        acc[1, self.head] = total.astype(BF16)
        self.n_up.append(w.send(acc.at[1, self.head], self.from_near.at[0, self.head], me.up))
        self.f_down.wait_recv()
        total = acc[2, self.tail].astype(F32) + self.from_far[1].astype(F32)
        acc[2, self.tail] = total.astype(BF16)
        self.n_down.append(w.send(acc.at[2, self.tail], self.from_near.at[1, self.tail], me.down))

    def result(self):
        self.cores[3].wait_recv()
        own = self.part[self.me.y * 2 + self.me.c]
        total = own.astype(F32) + self.from_core[3].astype(F32)
        arrived(self.n_up)
        arrived(self.n_down)
        return total + self.from_near[0].astype(F32) + self.from_near[1].astype(F32)


def full_row(pv_all, row):
    return jnp.concatenate(
        [pv_all[f].astype(F32)[row : row + 1, :] for f in range(8)], axis=1
    )


def columns(pv_all, f):
    tile = jnp.concatenate([pv_all[f].astype(F32), jnp.zeros((112, 128), F32)], axis=0)
    return tile.T


def norm_stats(values):
    mean_val = jnp.mean(values, axis=-1, keepdims=True)
    centered = values - mean_val
    variance = jnp.mean(centered * centered, axis=-1, keepdims=True)
    inverse = lax.rsqrt(variance + NORM_EPS)
    return centered * inverse, inverse


def norm_back(cotangent, gain, normed, inverse):
    scaled = cotangent * gain
    first = jnp.mean(scaled, axis=-1, keepdims=True)
    second = jnp.mean(scaled * normed, axis=-1, keepdims=True)
    return inverse * (scaled - first - normed * second)


def column_sum(values):
    return jnp.sum(values, axis=0, keepdims=True)


def half_of(which, pair):
    return jnp.where(which == 0, pair[:, :64], pair[:, 64:])


def beside(which, half):
    zero = jnp.zeros_like(half)
    return jnp.where(
        which == 0,
        jnp.concatenate([half, zero], axis=1),
        jnp.concatenate([zero, half], axis=1),
    )


def fold(piece):
    return jnp.concatenate([piece[:64], piece[64:]], axis=1)


def unfold(packed):
    return jnp.concatenate([packed[:, :64], packed[:, 64:]], axis=0)


def three_parts(values):
    first = values.astype(BF16)
    rest = values - first.astype(F32)
    second = rest.astype(BF16)
    third = (rest - second.astype(F32)).astype(BF16)
    return first.astype(F32), second.astype(F32), third.astype(F32)


def eight(ref):
    total = ref[0].astype(F32)
    for f in range(1, 8):
        total = total + ref[f].astype(F32)
    return total


def layer(
    tok, gout, valid, w_qkv, w_proj, w_fc1, w_fc2, gain_in, shift_in, scale_in, bias_in,
    res, gtok, gq, gp, w1_all, w2_all, o_vec,
    nrm, grd, pv_all, v_all, wq_one, wq_all, wq_use, wp_all, w1_one, wqf,
    qa, ka, va, ow, om, at,
    nmg, act, gpre, gn, mp, r_core, r_far, r_near, msg, gat, mid, gmid, atg, gac, gh,
    dw1, dw2, vec, db1,
    ga, qb, kt, dk, dv, dqt, wqt, qm, qin, kvm, kvin, m_core, m_far, m_near,
    dwp, r1, r2, rp, x1, x2, xp, dwq, rq, vs, vr, vq,
    ss, rs, as_, ar_, bs, br, own_sem,
):
    me = Place()
    wire = Wire(ss, rs)
    greet(me)
    normed, _ = norm_stats(tok[...].astype(F32))
    nrm[me.s] = normed.astype(BF16)
    v_all[me.s] = jnp.broadcast_to(valid[...].astype(F32), (16, 128)).astype(BF16)
    bias = half_of(me.c, bias_in[:, lanes(me.y * 128)].astype(F32))
    pv_all[me.f] = jnp.concatenate(
        [
            gain_in[...].astype(F32),
            shift_in[...].astype(F32),
            scale_in[...].astype(F32),
            jnp.concatenate([bias, jnp.zeros((1, 64), F32)], axis=1),
            jnp.zeros((5, 128), F32),
        ],
        axis=0,
    ).astype(BF16)
    parts = [half_of(me.c, w_qkv[:, lanes(p * 1024 + me.chip * 128)]) for p in range(3)]
    wq_one[...] = jnp.concatenate([*parts, jnp.zeros((128, 64), BF16)], axis=1)
    all_met()

    gather = Gather16(wire, me, nrm)
    gather.start()
    own_pv = pv_all.at[me.f]
    got_pv = to_fsdp(wire, me, lambda p: own_pv, lambda f: pv_all.at[f])
    got_wq = to_fsdp(wire, me, lambda p: wq_one, lambda f: wq_all.at[f])
    got_v = []
    for step in range(1, 16):
        peer = (me.s + step) % 16
        got_v.append(wire.send(v_all.at[me.s], v_all.at[me.s], (me.f, peer)))
    half = pl.ds(pl.multiple_of(me.c * 64, 64), 64)

    wq_all[me.f] = wq_one[...]
    for f in range(0, 8, 2):
        pair = [half_of(me.c, w_fc1[:, lanes(g * 512 + me.y * 128)]) for g in (f, f + 1)]
        w1_one[:, f * 64 : (f + 2) * 64] = jnp.concatenate(pair, axis=1)
    w1_all[me.f] = w1_one[...]
    own_wp = pltpu.make_async_copy(w_proj, wp_all.at[me.f], own_sem.at[0])
    own_wp.start()
    wqf[me.f] = w_qkv[...]
    mine = pl.ds(pl.multiple_of(me.j * 64, 64), 64)
    own_w2 = pltpu.make_async_copy(w_fc2.at[mine], w2_all.at[me.f], own_sem.at[1])
    own_w2.start()
    ready = {}

    fan_w1 = Fan(wire, me, w1_one, lambda f: w1_all.at[f])
    fan_w2 = Fan(wire, me, w_fc2.at[mine], lambda f: w2_all.at[f])
    fan_wqf = Fan(wire, me, w_qkv.at[half], lambda f: wqf.at[f, half])

    def more_weights():
        own_wp.wait()
        own_w2.wait()
        ready["wp"] = to_fsdp(
            wire, me, lambda p: w_proj.at[half], lambda f: wp_all.at[f, half]
        )
        fan_w1.start()
        fan_w2.start()

    def prepare():
        arrived(got_pv)
        arrived(got_wq)
        shifts = jnp.zeros((1, 256), F32)
        for f in range(8):
            cols = columns(pv_all, f)
            weight = wq_all[f]
            wq_use[f * 128 : (f + 1) * 128, :] = (weight.astype(F32) * cols[:, 0:1]).astype(BF16)
            row = jnp.broadcast_to(pv_all[f].astype(F32)[2:3, :], (16, 128)).astype(BF16)
            shifts = shifts + dot(row, weight)[0:1]
        own = half_of(me.c, pv_all[me.chip].astype(F32))
        zero = jnp.zeros((1, 64), F32)
        ready["bias"] = shifts + jnp.concatenate([own[4:5], zero, own[5:6], zero], axis=1)
        arrived(got_v)
        flags = v_all[:, 0, :].astype(F32)
        flags = jnp.concatenate([flags, jnp.zeros((112, 128), F32)], axis=0).T
        lane = lax.broadcasted_iota(jnp.int32, (128, 64), 1)
        for blk in range(16):
            mask = (1.0 - flags[:, blk : blk + 1]) * NEG_FILL
            ext = jnp.where(lane == 0, mask, jnp.where(lane < 4, 1.0, 0.0))
            ka[blk * 128 : (blk + 1) * 128, 64:] = ext.astype(BF16)

    ext_lane = lax.broadcasted_iota(jnp.int32, (128, 64), 1)
    q_ext = jnp.where(ext_lane == 0, 1.0, 0.0).astype(BF16)
    v_ext = jnp.where(ext_lane < 3, 1.0, 0.0).astype(BF16)

    def project(slot):
        qkv = dot(nrm[slot], wq_use[...]) + ready["bias"]
        rows = pl.ds(pl.multiple_of(slot * 128, 128), 128)
        query = (qkv[:, :64].astype(BF16) * 0.125).astype(BF16)
        qa[rows, :] = jnp.concatenate([query, q_ext], axis=1)
        ka[rows, :64] = qkv[:, 64:128].astype(BF16)
        va[rows, :] = jnp.concatenate([qkv[:, 128:192].astype(BF16), v_ext], axis=1)

    gather.run(more_weights, prepare, project)
    grd[me.j] = (full_row(pv_all, 9) * gout[...].astype(F32)).astype(BF16)
    grad_gather = Gather8(wire, me, grd)
    grad_gather.start()

    heads_out = Scatter(me, as_, ar_, om, at)
    out_lane = lax.broadcasted_iota(jnp.int32, (256, 128), 1)

    def attend(k):
        chip = (me.chip + 1 + k) % 8
        rows = pl.ds(pl.multiple_of(chip * 256, 256), 256)
        scores = dot(qa[rows, :], ka[...], NT)
        row_max = jnp.max(scores, axis=1, keepdims=True)
        terms = jnp.exp(scores - row_max).astype(BF16)
        mixed = dot(terms, va[...])
        total = mixed[:, 64:65]
        heads = mixed / total
        log_sum = row_max + jnp.log(total)
        ow[rows, :] = jnp.where(out_lane < 64, heads, log_sum)
        rounded = heads[:, :64].astype(BF16)
        for e in range(2):
            om[chip * 2 + e] = fold(rounded[e * 128 : (e + 1) * 128])

    def attend_send(k, carry):
        attend(k)
        heads_out.send(k)
        return carry

    fan_w1.relay_near()
    fan_w2.relay_near()
    lax.fori_loop(0, 2, attend_send, 0)
    grad_gather.relay()
    fan_w1.relay_far()
    fan_w2.relay_far()
    lax.fori_loop(2, 5, attend_send, 0)
    grad_gather.middle()
    lax.fori_loop(5, 7, attend_send, 0)
    grad_gather.last()
    arrived(ready["wp"])
    swap = [wire.send(wp_all.at[f, half], wp_all.at[f, half], me.core) for f in range(8)]
    fan_wqf.start()
    attend(7)
    heads_out.keep(wire)
    heads_out.finish()

    attn_tok = jnp.concatenate([unfold(at[h]) for h in range(16)], axis=1)
    atg[me.j] = attn_tok
    arrived(swap)
    scale_one = full_row(pv_all, 8)
    branch = dot(attn_tok, wp_all[...].reshape(1024, 1024)) + full_row(pv_all, 6)
    middle = tok[...].astype(F32) + scale_one * branch
    mid[...] = middle
    normed, inverse = norm_stats(middle)
    gain = full_row(pv_all, 1)
    nmg[me.j] = (normed * gain + full_row(pv_all, 3)).astype(BF16)
    gather = Gather8(wire, me, nmg)
    gather.start()
    attn_gather = Gather8(wire, me, atg)
    grad_gather.finish()
    gather.relay()
    gather.middle()
    attn_gather.start()
    gather.last()
    fan_w1.finish()
    fan_w2.finish()
    fan_wqf.relay_near()
    bias_one = jnp.concatenate(
        [pv_all[f].astype(F32)[10:11, :64] for f in range(8)], axis=1
    )
    gather.finish()

    def feed(b, carry):
        two = pl.ds(2 * b, 2)
        rows = pl.ds(pl.multiple_of(b * 256, 256), 256)
        w1 = w1_all[...].reshape(1024, 512)
        w2 = w2_all[...].reshape(512, 1024)
        pre = dot(nmg[two].reshape(256, 1024), w1) + bias_one
        cdf = 0.5 * (1.0 + lax.erf(pre * 0.7071067811865476))
        acts = (pre * cdf).astype(BF16)
        act[rows, :] = acts
        mp[two] = dot(acts, w2).astype(BF16).reshape(2, 128, 1024)
        grad_act = dot(grd[two].reshape(256, 1024), w2, NT)
        slope = cdf + pre * jnp.exp(-0.5 * pre * pre) * 0.3989422804014327
        grad_pre = (grad_act * slope).astype(BF16)
        gpre[rows, :] = grad_pre
        gn[two] = dot(grad_pre, w1, NT).astype(BF16).reshape(2, 128, 1024)
        return carry + column_sum(grad_pre.astype(F32))

    db1[...] = lax.fori_loop(0, 4, feed, jnp.zeros((1, 512), F32))
    fan_w1.settle()
    fan_w2.settle()
    reduce = Reduce8(wire, me, gn, r_core, r_far, r_near)
    reduce.start()
    fan_wqf.relay_far()
    reduce.far()
    attn_gather.relay()
    dw2[...] = dot(act[...], grd[...].reshape(1024, 1024), TN).astype(BF16).reshape(8, 64, 1024)
    reduce.near()
    fan_dw2 = FanIn(wire, me, dw2, r2)
    fan_dw2.start()
    dw1[...] = dot(nmg[...].reshape(1024, 1024), gpre[...], TN).astype(BF16).reshape(8, 128, 512)
    fan_dw1 = FanIn(wire, me, dw1, r1)
    fan_dw1.start()
    cotangent = reduce.result()
    grad_middle = gout[...].astype(F32) + norm_back(cotangent, gain, normed, inverse)
    gmid[...] = grad_middle
    grad_attn = (scale_one * grad_middle).astype(BF16)
    gat[...] = grad_attn
    grad_tok = dot(grad_attn, wp_all[...].reshape(1024, 1024), NT).astype(BF16)
    for h in range(16):
        msg[h] = fold(grad_tok[:, h * 64 : (h + 1) * 64])
    gh[me.s] = msg[me.s]
    got_gh = []
    for step in range(1, 16):
        peer = (me.s + step) % 16
        got_gh.append(wire.send(msg.at[peer], gh.at[me.s], (me.f, peer)))
    got_gac = []
    for step in range(1, 8):
        peer = (me.j + step) % 8
        device = (me.f, me.slot(peer // 2, me.xl, peer % 2))
        got_gac.append(wire.send(gat.at[:, lanes(peer * 128)], gac.at[me.j], device))
    gac[me.j] = gat[:, lanes(me.j * 128)]
    mlp = Reduce8(wire, me, mp, m_core, m_far, m_near)
    mlp.start()
    zero = jnp.zeros((1, 1024), F32)
    vec[...] = jnp.concatenate(
        [
            zero,
            column_sum(cotangent * normed),
            zero,
            column_sum(cotangent),
            zero,
            zero,
            column_sum(grad_attn.astype(F32)),
            column_sum(grd[me.j].astype(F32)),
            column_sum(grad_middle * branch),
            jnp.zeros((7, 1024), F32),
        ],
        axis=0,
    )
    attn_gather.middle()
    attn_gather.last()
    mlp.far()
    lane = lax.broadcasted_iota(jnp.int32, (128, 128), 1)
    for blk in range(16):
        rows = slice(blk * 128, (blk + 1) * 128)
        l1, l2, l3 = three_parts(-ow[rows, 64:65])
        wide = qa[rows, :].astype(F32)
        wide = jnp.where(lane == 65, l1, wide)
        wide = jnp.where(lane == 66, l2, wide)
        wide = jnp.where(lane == 67, l3, wide)
        qb[rows, :] = wide.astype(BF16)
        kt[:, rows] = ka[rows, :].astype(F32).T.astype(BF16)
    for f in range(8):
        weight = wq_all[f].astype(F32)
        wqt[f, :128] = weight[:, :128].T.astype(BF16)
        wqt[f, 128:] = weight[:, 128:].T[:64].astype(BF16)
    dk[...] = jnp.zeros_like(dk)
    dv[...] = jnp.zeros_like(dv)

    arrived(got_gh)
    for blk in range(16):
        rows = slice(blk * 128, (blk + 1) * 128)
        grad = unfold(gh[blk])
        delta = jnp.sum(grad.astype(F32) * ow[rows, :64], axis=1, keepdims=True)
        d1, d2, d3 = three_parts(-delta)
        wide = jnp.concatenate([grad, jnp.zeros((128, 64), BF16)], axis=1).astype(F32)
        wide = jnp.where(lane == 64, d1, wide)
        wide = jnp.where(lane == 65, d2, wide)
        wide = jnp.where(lane == 66, d3, wide)
        ga[rows, :] = wide.astype(BF16)

    queries_out = Scatter(me, bs, br, qm, qin)

    def back(k):
        chip = (me.chip + 1 + k) % 8
        rows = pl.ds(pl.multiple_of(chip * 256, 256), 256)
        query, grad = qb[rows, :], ga[rows, :]
        probs = jnp.exp(dot(ka[...], query, NT))
        dv[...] += dot(probs.astype(BF16), grad)
        slope = dot(va[...], grad, NT)
        scores = (probs * slope).astype(BF16)
        dk[...] += dot(scores, query)
        turned = dot(kt[...], scores)
        grad_query = (turned.T[:, :64] * 0.125).astype(BF16)
        dqt[:64, rows] = (turned[:64] * 0.125).astype(BF16)
        for e in range(2):
            qm[chip * 2 + e] = fold(grad_query[e * 128 : (e + 1) * 128])

    def back_send(k, carry):
        back(k)
        queries_out.send(k)
        return carry

    lax.fori_loop(0, 3, back_send, 0)
    mlp.near()
    arrived(got_gac)
    attn_gather.finish()
    for f in range(8):
        tok_cols = atg[:, :, f * 128 : (f + 1) * 128].reshape(1024, 128)
        dwp[f] = dot(tok_cols, gac[...].reshape(1024, 128), TN).astype(BF16)
    fan_dw2.forward()
    fan_dw1.forward()
    got = to_fsdp(wire, me, lambda p: dwp.at[p], lambda f: rp.at[f])
    rp[me.f] = dwp[me.f]
    lax.fori_loop(3, 6, back_send, 0)
    fan_wqf.finish()
    swap = [wire.send(wqf.at[f, half], wqf.at[f, half], me.core) for f in range(8)]
    lax.fori_loop(6, 7, back_send, 0)
    back(7)
    queries_out.keep(wire)

    for blk in range(16):
        rows = slice(blk * 128, (blk + 1) * 128)
        grad_key, grad_value = dk[rows, :64].astype(BF16), dv[rows, :64].astype(BF16)
        pair = jnp.concatenate([grad_key, grad_value], axis=1)
        kvm[blk] = pair
        dqt[64:, rows] = pair.astype(F32).T.astype(BF16)
    got_kv = []
    for step in range(1, 16):
        peer = (me.s + step) % 16
        got_kv.append(wire.send(kvm.at[peer], kvin.at[me.s], (me.f, peer)))
    kvin[me.s] = kvm[me.s]

    arrived(got)
    x1[0] = fan_dw1.result().astype(BF16)
    x2[0] = fan_dw2.result().astype(BF16)
    xp[0] = eight(rp).astype(BF16)
    crossed = [wire.send(x.at[0], x.at[1], me.xpart) for x in (x1, x2, xp)]

    mlp_out = mlp.result() + full_row(pv_all, 7)
    res[...] = (mid[...] + full_row(pv_all, 9) * mlp_out).astype(BF16)
    vec[9:10, :] = column_sum(gout[...].astype(F32) * mlp_out)
    sums = jnp.sum(dqt[...].astype(F32), axis=1, keepdims=True)
    turned = jnp.broadcast_to(sums, (192, 128))
    turned = jnp.concatenate([turned, jnp.zeros((64, 128), F32)], axis=0)
    sum_q, sum_v = turned[:128].T[0:1, :64], turned[128:].T[0:1, :64]
    got_q, got_vec = [], []
    for step in range(1, 9):
        f = (me.f + step) % 8
        own = pv_all[f].astype(F32)
        product = dot(dqt[...], nrm[:, :, lanes(f * 128)].reshape(2048, 128))
        grad_wq = product * own[0:1] + sums * own[2:3]
        weight = wqt[f].astype(F32)
        rows = vec[:, lanes(f * 128)]
        piece = half_of(f % 2, db1[:, lanes((f // 2) * 128)])
        bias = beside(me.c, piece)
        here = me.chip == f
        packed = jnp.concatenate(
            [
                column_sum(weight * product),
                rows[1:2],
                column_sum(weight * sums),
                rows[3:4],
                jnp.where(here, beside(me.c, sum_q), 0.0),
                jnp.where(here, beside(me.c, sum_v), 0.0),
                rows[6:10],
                *[jnp.where(me.y == y, bias, 0.0) for y in range(4)],
                jnp.zeros((2, 128), F32),
            ],
            axis=0,
        )
        if step < 8:
            dwq[f] = grad_wq.astype(BF16)
            vs[f] = packed
            got_q.append(wire.send(dwq.at[f], rq.at[me.f], (f, me.s)))
            got_vec.append(wire.send(vs.at[f], vr.at[me.f], (f, me.s)))
        else:
            rq[me.f] = grad_wq.astype(BF16)
            vr[me.f] = packed

    arrived(crossed)
    gathers = []
    for x, g in ((x1, w1_all), (x2, w2_all), (xp, gp)):
        g[me.j] = (x[0].astype(F32) + x[1].astype(F32)).astype(BF16)
        gathers.append(Gather8(wire, me, g))
    for gather in gathers:
        gather.start()

    queries_out.finish()
    arrived(got_kv)
    arrived(swap)
    parts = [unfold(qin[h]) for h in range(16)]
    parts += [kvin[h][:, :64] for h in range(16)] + [kvin[h][:, 64:] for h in range(16)]
    grad_qkv = jnp.concatenate(parts, axis=1)
    cotangent = dot(grad_qkv, wqf[...].reshape(1024, 3072), NT)

    arrived(got_q)
    gq[me.s] = eight(rq).astype(BF16)
    gather_q = Gather16(wire, me, gq)
    gather_q.start()
    arrived(got_vec)
    vq[me.s] = eight(vr)
    got_vq = []
    for step in range(1, 16):
        peer = (me.s + step) % 16
        got_vq.append(wire.send(vq.at[me.s], vq.at[me.s], (me.f, peer)))
    for gather in gathers:
        gather.relay()
    for gather in gathers:
        gather.middle()
    normed, inverse = norm_stats(tok[...].astype(F32))
    gtok[...] = gmid[...] + norm_back(cotangent, full_row(pv_all, 0), normed, inverse)
    for gather in gathers:
        gather.last()
    gather_q.run()
    for gather in gathers:
        gather.finish()
    arrived(got_vq)
    total = vq[0]
    for s in range(1, 16):
        total = total + vq[s]
    o_vec[...] = total
    wire.drain()


OUTS = (
    ((128, 1024), BF16),
    ((128, 1024), F32),
    ((16, 192, 128), BF16),
    ((8, 128, 128), BF16),
    ((8, 128, 512), BF16),
    ((8, 64, 1024), BF16),
    ((16, 128), F32),
)
GRADS = (
    ((128, 1024), BF16),
    ((128, 1024), F32),
    ((128, 3072), F32),
    ((128, 1024), F32),
    ((128, 4096), F32),
    ((512, 1024), F32),
    ((2, 128), F32),
    ((6, 128), F32),
    ((2, 128), F32),
    ((4, 128), F32),
)


def lay_out(res, gtok, gq, gp, g1, g2, vec, o_res, o_tok, o_qkv, o_proj, o_fc1, o_fc2, *o_vecs):
    o_res[...] = res[...]
    o_tok[...] = gtok[...]
    for part in range(3):
        rows = slice(part * 64, (part + 1) * 64)
        for k in range(8):
            pair = jnp.concatenate([gq[2 * k, rows, :], gq[2 * k + 1, rows, :]], axis=0)
            at = part * 1024 + k * 128
            o_qkv[:, at : at + 128] = pair.astype(F32).T
    for j in range(8):
        o_proj[:, j * 128 : (j + 1) * 128] = gp[j].astype(F32)
        o_fc2[j * 64 : (j + 1) * 64, :] = g2[j].astype(F32)
    for f in range(8):
        cols = slice(f * 64, (f + 1) * 64)
        for k in range(4):
            pair = jnp.concatenate([g1[2 * k, :, cols], g1[2 * k + 1, :, cols]], axis=1)
            at = f * 512 + k * 128
            o_fc1[:, at : at + 128] = pair.astype(F32)
    row = 0
    for out in o_vecs:
        out[...] = vec[row : row + out.shape[0], :]
        row += out.shape[0]


SCRATCH = (
    ((16, 128, 1024), BF16),
    ((8, 128, 1024), BF16),
    ((8, 16, 128), BF16),
    ((16, 16, 128), BF16),
    ((128, 256), BF16),
    ((8, 128, 256), BF16),
    ((1024, 256), BF16),
    ((8, 128, 1024), BF16),
    ((128, 512), BF16),
    ((8, 128, 3072), BF16),
    ((2048, 128), BF16),
    ((2048, 128), BF16),
    ((2048, 128), BF16),
    ((2048, 128), F32),
    ((16, 64, 128), BF16),
    ((16, 64, 128), BF16),
    ((8, 128, 1024), BF16),
    ((1024, 512), BF16),
    ((1024, 512), BF16),
    ((8, 128, 1024), BF16),
    ((8, 128, 1024), BF16),
    ((4, 128, 1024), BF16),
    ((2, 64, 1024), BF16),
    ((2, 128, 1024), BF16),
    ((16, 64, 128), BF16),
    ((128, 1024), BF16),
    ((128, 1024), F32),
    ((128, 1024), F32),
    ((8, 128, 1024), BF16),
    ((8, 128, 128), BF16),
    ((16, 64, 128), BF16),
    ((8, 128, 512), BF16),
    ((8, 64, 1024), BF16),
    ((16, 1024), F32),
    ((1, 512), F32),
    ((2048, 128), BF16),
    ((2048, 128), BF16),
    ((128, 2048), BF16),
    ((2048, 128), F32),
    ((2048, 128), F32),
    ((192, 2048), BF16),
    ((8, 192, 128), BF16),
    ((16, 64, 128), BF16),
    ((16, 64, 128), BF16),
    ((16, 128, 128), BF16),
    ((16, 128, 128), BF16),
    ((4, 128, 1024), BF16),
    ((2, 64, 1024), BF16),
    ((2, 128, 1024), BF16),
    ((8, 128, 128), BF16),
    ((8, 128, 512), BF16),
    ((8, 64, 1024), BF16),
    ((8, 128, 128), BF16),
    ((2, 128, 512), BF16),
    ((2, 64, 1024), BF16),
    ((2, 128, 128), BF16),
    ((8, 192, 128), BF16),
    ((8, 192, 128), BF16),
    ((8, 16, 128), F32),
    ((8, 16, 128), F32),
    ((16, 16, 128), F32),
)
COPIES = 352


def body(
    tokens, image_ids, valid, w_qkv, w_proj, w_fc1, w_fc2,
    norm_gain, shifts, layer_scale, fc1_bias, grad_out,
):
    semaphores = [pltpu.SemaphoreType.DMA((n,)) for n in (COPIES, COPIES, 14, 14, 14, 14, 2)]
    whole = pl.BlockSpec(memory_space=pltpu.VMEM)
    held = pl.BlockSpec(memory_space=pl.ANY)
    shares = pl.pallas_call(
        layer,
        out_shape=[jax.ShapeDtypeStruct(shape, dtype) for shape, dtype in OUTS],
        in_specs=[whole] * 4 + [held, whole, held] + [whole] * 4,
        out_specs=[whole] * len(OUTS),
        scratch_shapes=[pltpu.VMEM(shape, dtype) for shape, dtype in SCRATCH] + semaphores,
        name="layer",
        compiler_params=pltpu.CompilerParams(
            collective_id=1, has_side_effects=True, vmem_limit_bytes=VMEM_LIMIT
        ),
    )(
        tokens, grad_out, valid.reshape(1, 128), w_qkv[0], w_proj[0], w_fc1[0], w_fc2[0],
        norm_gain[0], shifts[0], layer_scale[0], fc1_bias,
    )
    outs = pl.pallas_call(
        lay_out,
        out_shape=[jax.ShapeDtypeStruct(shape, dtype) for shape, dtype in GRADS],
        in_specs=[whole] * len(OUTS),
        out_specs=[whole] * len(GRADS),
        name="lay_out",
        compiler_params=pltpu.CompilerParams(vmem_limit_bytes=VMEM_LIMIT),
    )(*shares)
    return (*outs[:2], *[out[None] for out in outs[2:9]], outs[9].reshape(1, 512))


def solution(mesh):
    rows = P(("fsdp", "seq"), None)
    flat = P(("fsdp", "seq"))
    mats = P(None, "fsdp", None)
    vecs = P(None, None, "fsdp")
    bias = P(None, "fsdp")
    return jax.shard_map(
        body,
        mesh=mesh,
        in_specs=(rows, flat, flat, mats, mats, mats, mats, vecs, vecs, vecs, bias, rows),
        out_specs=(rows, rows, mats, mats, mats, mats, vecs, vecs, vecs, bias),
        check_vma=False,
    )
```

```python
import jax
import jax.numpy as jnp
from jax import lax
from jax.experimental import pallas as pl
from jax.experimental.pallas import tpu as pltpu
from jax.sharding import PartitionSpec as P

NORM_EPS = 1e-06
NEG_FILL = -1e30
F32 = jnp.float32
BF16 = jnp.bfloat16
MESH = pl.DeviceIdType.MESH
NT = (((1,), (1,)), ((), ()))
TN = (((0,), (0,)), ((), ()))
NN = (((1,), (0,)), ((), ()))
VMEM_LIMIT = 63 * 1024 * 1024


def dot(left, right, dims=NN):
    return lax.dot_general(left, right, dims, preferred_element_type=F32)


def lanes(start, size=128):
    return pl.ds(pl.multiple_of(start, 128), size)


class Place:
    def __init__(self):
        self.f = lax.axis_index("fsdp")
        self.s = lax.axis_index("seq")
        self.y = self.s // 4
        self.xl = (self.s // 2) % 2
        self.c = self.s % 2
        self.yp = (self.y + 1) % 4
        self.ym = (self.y + 3) % 4
        self.yo = (self.y + 2) % 4
        self.chip = self.s // 2
        self.j = self.y * 2 + self.c
        self.core = (self.f, self.slot(self.y, self.xl, 1 - self.c))
        self.xpart = (self.f, self.slot(self.y, 1 - self.xl, self.c))
        self.up = (self.f, self.slot(self.yp, self.xl, self.c))
        self.down = (self.f, self.slot(self.ym, self.xl, self.c))

    def slot(self, y, xl, c):
        return (y * 2 + xl) * 2 + c


def greet(me):
    barrier = pltpu.get_barrier_semaphore()
    for step in range(1, 8):
        pl.semaphore_signal(
            barrier, inc=1, device_id=((me.f + step) % 8, me.s), device_id_type=MESH
        )
    for step in range(1, 16):
        pl.semaphore_signal(
            barrier, inc=1, device_id=(me.f, (me.s + step) % 16), device_id_type=MESH
        )


def all_met():
    pl.semaphore_wait(pltpu.get_barrier_semaphore(), 22)


class Wire:
    def __init__(self, send_sem, recv_sem):
        self.send_sem, self.recv_sem = send_sem, recv_sem
        self.used = 0
        self.sent = []

    def send(self, src, dst, device):
        k = self.used
        self.used += 1
        copy = pltpu.make_async_remote_copy(
            src_ref=src,
            dst_ref=dst,
            send_sem=self.send_sem.at[k],
            recv_sem=self.recv_sem.at[k],
            device_id=device,
            device_id_type=MESH,
        )
        copy.start()
        self.sent.append(copy)
        return copy

    def settle(self, copies):
        for copy in copies:
            copy.wait_send()
        done = {id(copy) for copy in copies}
        self.sent = [copy for copy in self.sent if id(copy) not in done]

    def drain(self):
        self.settle(list(self.sent))


class Scatter:
    def __init__(self, me, send_sem, recv_sem, out, into):
        self.me, self.out, self.into = me, out, into
        self.send_sem, self.recv_sem = send_sem, recv_sem

    def copy(self, k, e, peer, arriving):
        return pltpu.make_async_remote_copy(
            src_ref=self.out.at[peer],
            dst_ref=self.into.at[peer if arriving else self.me.s],
            send_sem=self.send_sem.at[2 * k + e],
            recv_sem=self.recv_sem.at[2 * k + (e if arriving else self.me.c)],
            device_id=(self.me.f, peer),
            device_id_type=MESH,
        )

    def send(self, k):
        chip = (self.me.chip + 1 + k) % 8
        self.copy(k, 0, chip * 2, False).start()
        self.copy(k, 1, chip * 2 + 1, False).start()

    def keep(self, wire):
        me = self.me
        self.into[me.s] = self.out[me.s]
        other = me.s + 1 - 2 * me.c
        self.partner = wire.send(self.out.at[other], self.into.at[me.s], me.core)

    def finish(self):
        def collect(k, carry):
            there, back = (self.me.chip + 1 + k) % 8, (self.me.chip + 7 - k) % 8
            for e in range(2):
                self.copy(k, e, there * 2 + e, False).wait_send()
                self.copy(k, e, back * 2 + e, True).wait_recv()
            return carry

        lax.fori_loop(0, 7, collect, 0)
        self.partner.wait_recv()


def to_fsdp(wire, me, src_of, dst_of):
    copies = []
    for step in range(1, 8):
        peer = (me.f + step) % 8
        copies.append(wire.send(src_of(peer), dst_of(me.f), (peer, me.s)))
    return copies


def arrived(copies):
    for copy in copies:
        copy.wait_recv()


class Fan:
    def __init__(self, wire, me, src, dst):
        self.wire, self.me, self.src, self.dst = wire, me, src, dst

    def at(self, dz, other=False):
        z, xh = self.me.f // 2, self.me.f % 2
        return ((z + dz) % 4) * 2 + (1 - xh if other else xh)

    def push(self, src, dst, f):
        return self.wire.send(src, dst, (f, self.me.s))

    def start(self):
        slot = self.dst(self.me.f)
        self.cross = self.push(self.src, slot, self.at(0, True))
        self.near = [self.push(self.src, slot, self.at(dz)) for dz in (1, 3)]
        self.far = self.push(self.src, slot, self.at(2))

    def relay_near(self):
        self.cross.wait_recv()
        slot = self.dst(self.at(0, True))
        self.near += [self.push(slot, slot, self.at(dz)) for dz in (1, 3)]

    def relay_far(self):
        self.far.wait_recv()
        slot = self.dst(self.at(2))
        self.near.append(self.push(slot, slot, self.at(0, True)))

    def finish(self):
        arrived(self.near)

    def settle(self):
        self.wire.settle([self.cross, self.far, *self.near])


class FanIn(Fan):
    def __init__(self, wire, me, part, into):
        self.wire, self.me, self.part, self.into = wire, me, part, into

    def start(self):
        part, into = self.part, self.into
        self.over = [self.push(part.at[self.at(2, True)], into.at[6], self.at(0, True))]
        for k, dz in enumerate((1, 3)):
            self.over.append(self.push(part.at[self.at(dz, True)], into.at[4 + k], self.at(dz)))
        self.last = []
        for k, dz in enumerate((1, 3)):
            self.last.append(self.push(part.at[self.at(dz)], into.at[1 + k], self.at(dz)))

    def forward(self):
        part, into = self.part, self.into
        arrived(self.over)
        total = into[4].astype(F32) + into[5].astype(F32) + part[self.at(0, True)].astype(F32)
        into[4] = total.astype(BF16)
        self.last.append(self.push(into.at[4], into.at[0], self.at(0, True)))
        total = into[6].astype(F32) + part[self.at(2)].astype(F32)
        into[6] = total.astype(BF16)
        self.last.append(self.push(into.at[6], into.at[3], self.at(2)))

    def result(self):
        arrived(self.last)
        total = self.part[self.me.f].astype(F32)
        for k in range(4):
            total = total + self.into[k].astype(F32)
        return total


class Gather8:
    def __init__(self, wire, me, ref):
        self.wire, self.me, self.ref = wire, me, ref
        h = ref.shape[1] // 2
        self.head, self.tail = pl.ds(0, h), pl.ds(h, h)

    def slot(self, y):
        return y * 2 + self.me.c

    def push(self, y, part, device):
        at = self.ref.at[self.slot(y)] if part is None else self.ref.at[self.slot(y), part]
        return self.wire.send(at, at, device)

    def start(self):
        me = self.me
        self.up = [self.push(me.y, self.head, me.up)]
        self.down = [self.push(me.y, self.tail, me.down)]
        self.up.append(self.push(me.y, self.tail, me.up))
        self.down.append(self.push(me.y, self.head, me.down))
        self.cores = [self.push(me.y, None, me.core)]

    def relay(self):
        me = self.me
        self.up[0].wait_recv()
        self.far = [self.push(me.ym, self.head, me.up)]
        self.down[0].wait_recv()
        self.far.append(self.push(me.yp, self.tail, me.down))

    def middle(self):
        me = self.me
        self.up[1].wait_recv()
        self.cores.append(self.push(me.ym, None, me.core))
        self.down[1].wait_recv()
        self.cores.append(self.push(me.yp, None, me.core))

    def last(self):
        arrived(self.far)
        self.cores.append(self.push(self.me.yo, None, self.me.core))

    def finish(self):
        arrived(self.cores)


class Gather16:
    def __init__(self, wire, me, ref):
        self.wire, self.me, self.ref = wire, me, ref
        h = ref.shape[1] // 2
        self.head, self.tail = pl.ds(0, h), pl.ds(h, h)
        self.cores = []

    def slot(self, y, other):
        me = self.me
        return me.slot(y, 1 - me.xl if other else me.xl, me.c)

    def push(self, y, other, part, device):
        at = self.slot(y, other)
        at = self.ref.at[at] if part is None else self.ref.at[at, part]
        return self.wire.send(at, at, device)

    def to_core(self, y, other):
        self.cores.append((self.push(y, other, None, self.me.core), y, other))

    def spread(self, other):
        me = self.me
        up = [self.push(me.y, other, self.head, me.up)]
        down = [self.push(me.y, other, self.tail, me.down)]
        up.append(self.push(me.y, other, self.tail, me.up))
        down.append(self.push(me.y, other, self.head, me.down))
        return up, down

    def start(self):
        me = self.me
        self.cross = [self.push(me.y, False, part, me.xpart) for part in (self.head, self.tail)]
        self.near = [self.spread(False)]
        self.to_core(me.y, False)

    def relay(self, other):
        me = self.me
        up, down = self.near[int(other)]
        up[0].wait_recv()
        far = [self.push(me.ym, other, self.head, me.up)]
        down[0].wait_recv()
        far.append(self.push(me.yp, other, self.tail, me.down))
        return far

    def middle(self, other):
        up, down = self.near[int(other)]
        up[1].wait_recv()
        self.to_core(self.me.ym, other)
        down[1].wait_recv()
        self.to_core(self.me.yp, other)

    def run(self, crossed=lambda: None, prepare=lambda: None, use=lambda slot: None):
        me = self.me
        far_own = self.relay(False)
        arrived(self.cross)
        self.near.append(self.spread(True))
        self.to_core(me.y, True)
        crossed()
        self.middle(False)
        far_part = self.relay(True)
        arrived(far_own)
        self.to_core(me.yo, False)
        prepare()
        use(self.slot(me.y, False))
        use(self.slot(me.y, True))
        use(self.slot(me.ym, False))
        use(self.slot(me.yp, False))
        self.middle(True)
        use(self.slot(me.yo, False))
        for copy, y, other in self.cores[:3]:
            copy.wait_recv()
            use(me.slot(y, 1 - me.xl if other else me.xl, 1 - me.c))
        arrived(far_part)
        self.to_core(me.yo, True)
        use(self.slot(me.ym, True))
        use(self.slot(me.yp, True))
        use(self.slot(me.yo, True))
        for copy, y, other in self.cores[3:]:
            copy.wait_recv()
            use(me.slot(y, 1 - me.xl if other else me.xl, 1 - me.c))


class Reduce8:
    def __init__(self, wire, me, part, from_core, from_far, from_near):
        self.wire, self.me, self.part = wire, me, part
        self.from_core, self.from_far, self.from_near = from_core, from_far, from_near
        self.order = (me.yo, me.yp, me.ym, me.y)

        self.cores = {}
        h = from_core.shape[1] // 2
        self.head, self.tail = pl.ds(0, h), pl.ds(h, h)

    def start(self, d):
        src = self.part.at[self.order[d] * 2 + 1 - self.me.c]
        self.cores[d] = self.wire.send(src, self.from_core.at[d], self.me.core)

    def combine(self, d):
        self.cores[d].wait_recv()
        own = self.part[self.order[d] * 2 + self.me.c]
        total = own.astype(F32) + self.from_core[d].astype(F32)
        self.from_core[d] = total.astype(BF16)

    def far(self):
        w, me, acc = self.wire, self.me, self.from_core
        self.combine(0)
        self.f_up = w.send(acc.at[0, self.head], self.from_far.at[0], me.up)
        self.f_down = w.send(acc.at[0, self.tail], self.from_far.at[1], me.down)

    def near_halves(self):
        w, me, acc = self.wire, self.me, self.from_core
        self.combine(1)
        self.n_up = [w.send(acc.at[1, self.tail], self.from_near.at[0, self.tail], me.up)]
        self.combine(2)
        self.n_down = [w.send(acc.at[2, self.head], self.from_near.at[1, self.head], me.down)]

    def near(self):
        w, me, acc = self.wire, self.me, self.from_core
        self.f_up.wait_recv()
        total = acc[1, self.head].astype(F32) + self.from_far[0].astype(F32)
        acc[1, self.head] = total.astype(BF16)
        self.n_up.append(w.send(acc.at[1, self.head], self.from_near.at[0, self.head], me.up))
        self.f_down.wait_recv()
        total = acc[2, self.tail].astype(F32) + self.from_far[1].astype(F32)
        acc[2, self.tail] = total.astype(BF16)
        self.n_down.append(w.send(acc.at[2, self.tail], self.from_near.at[1, self.tail], me.down))

    def result(self):
        self.cores[3].wait_recv()
        own = self.part[self.me.y * 2 + self.me.c]
        total = own.astype(F32) + self.from_core[3].astype(F32)
        arrived(self.n_up)
        arrived(self.n_down)
        return total + self.from_near[0].astype(F32) + self.from_near[1].astype(F32)


def full_row(pv_all, row):
    return jnp.concatenate(
        [pv_all[f].astype(F32)[row : row + 1, :] for f in range(8)], axis=1
    )


def columns(pv_all, f):
    tile = jnp.concatenate([pv_all[f].astype(F32), jnp.zeros((112, 128), F32)], axis=0)
    return tile.T


def norm_stats(values):
    mean_val = jnp.mean(values, axis=-1, keepdims=True)
    centered = values - mean_val
    variance = jnp.mean(centered * centered, axis=-1, keepdims=True)
    inverse = lax.rsqrt(variance + NORM_EPS)
    return centered * inverse, inverse


def norm_back(cotangent, gain, normed, inverse):
    scaled = cotangent * gain
    first = jnp.mean(scaled, axis=-1, keepdims=True)
    second = jnp.mean(scaled * normed, axis=-1, keepdims=True)
    return inverse * (scaled - first - normed * second)


def column_sum(values):
    return jnp.sum(values, axis=0, keepdims=True)


def half_of(which, pair):
    return jnp.where(which == 0, pair[:, :64], pair[:, 64:])


def beside(which, half):
    zero = jnp.zeros_like(half)
    return jnp.where(
        which == 0,
        jnp.concatenate([half, zero], axis=1),
        jnp.concatenate([zero, half], axis=1),
    )


def fold(piece):
    return jnp.concatenate([piece[:64], piece[64:]], axis=1)


def unfold(packed):
    return jnp.concatenate([packed[:, :64], packed[:, 64:]], axis=0)


def three_parts(values):
    first = values.astype(BF16)
    rest = values - first.astype(F32)
    second = rest.astype(BF16)
    third = (rest - second.astype(F32)).astype(BF16)
    return first.astype(F32), second.astype(F32), third.astype(F32)


def eight(ref):
    total = ref[0].astype(F32)
    for f in range(1, 8):
        total = total + ref[f].astype(F32)
    return total


def layer(
    tok, gout, valid, w_qkv, w_proj, w_fc1, w_fc2, gain_in, shift_in, scale_in, bias_in,
    res, gtok, gq, gp, w1_all, w2_all, o_vec,
    nrm, grd, pv_all, v_all, wq_one, wq_all, wq_use, wp_all, w1_one, wqf,
    qa, ka, va, ow, om, at,
    nmg, act, gpre, gn, mp, r_core, r_far, r_near, msg, gat, mid, gmid, atg, gac, gh,
    dw1, dw2, vec, db1,
    ga, qb, kt, dk, dv, dqt, wqt, qm, qin, kvm, kvin, m_core, m_far, m_near,
    dwp, r1, r2, rp, x1, x2, xp, dwq, rq, vs, vr, vq,
    ss, rs, as_, ar_, bs, br, own_sem,
):
    me = Place()
    wire = Wire(ss, rs)
    greet(me)
    normed, _ = norm_stats(tok[...].astype(F32))
    nrm[me.s] = normed.astype(BF16)
    v_all[me.s] = jnp.broadcast_to(valid[...].astype(F32), (16, 128)).astype(BF16)
    bias = half_of(me.c, bias_in[:, lanes(me.y * 128)].astype(F32))
    pv_all[me.f] = jnp.concatenate(
        [
            gain_in[...].astype(F32),
            shift_in[...].astype(F32),
            scale_in[...].astype(F32),
            jnp.concatenate([bias, jnp.zeros((1, 64), F32)], axis=1),
            jnp.zeros((5, 128), F32),
        ],
        axis=0,
    ).astype(BF16)
    parts = [half_of(me.c, w_qkv[:, lanes(p * 1024 + me.chip * 128)]) for p in range(3)]
    wq_one[...] = jnp.concatenate([*parts, jnp.zeros((128, 64), BF16)], axis=1)
    all_met()

    gather = Gather16(wire, me, nrm)
    gather.start()
    own_pv = pv_all.at[me.f]
    got_pv = to_fsdp(wire, me, lambda p: own_pv, lambda f: pv_all.at[f])
    got_wq = to_fsdp(wire, me, lambda p: wq_one, lambda f: wq_all.at[f])
    got_v = []
    for step in range(1, 16):
        peer = (me.s + step) % 16
        got_v.append(wire.send(v_all.at[me.s], v_all.at[me.s], (me.f, peer)))
    half = pl.ds(pl.multiple_of(me.c * 64, 64), 64)

    wq_all[me.f] = wq_one[...]
    for f in range(0, 8, 2):
        pair = [half_of(me.c, w_fc1[:, lanes(g * 512 + me.y * 128)]) for g in (f, f + 1)]
        w1_one[:, f * 64 : (f + 2) * 64] = jnp.concatenate(pair, axis=1)
    w1_all[me.f] = w1_one[...]
    own_wp = pltpu.make_async_copy(w_proj, wp_all.at[me.f], own_sem.at[0])
    own_wp.start()
    wqf[me.f] = w_qkv[...]
    mine = pl.ds(pl.multiple_of(me.j * 64, 64), 64)
    own_w2 = pltpu.make_async_copy(w_fc2.at[mine], w2_all.at[me.f], own_sem.at[1])
    own_w2.start()
    ready = {}

    fan_w1 = Fan(wire, me, w1_one, lambda f: w1_all.at[f])
    fan_w2 = Fan(wire, me, w_fc2.at[mine], lambda f: w2_all.at[f])
    fan_wqf = Fan(wire, me, w_qkv.at[half], lambda f: wqf.at[f, half])

    def more_weights():
        own_wp.wait()
        own_w2.wait()
        ready["wp"] = to_fsdp(
            wire, me, lambda p: w_proj.at[half], lambda f: wp_all.at[f, half]
        )
        fan_w1.start()
        fan_w2.start()

    def prepare():
        arrived(got_pv)
        arrived(got_wq)
        shifts = jnp.zeros((1, 256), F32)
        for f in range(8):
            cols = columns(pv_all, f)
            weight = wq_all[f]
            wq_use[f * 128 : (f + 1) * 128, :] = (weight.astype(F32) * cols[:, 0:1]).astype(BF16)
            row = jnp.broadcast_to(pv_all[f].astype(F32)[2:3, :], (16, 128)).astype(BF16)
            shifts = shifts + dot(row, weight)[0:1]
        own = half_of(me.c, pv_all[me.chip].astype(F32))
        zero = jnp.zeros((1, 64), F32)
        ready["bias"] = shifts + jnp.concatenate([own[4:5], zero, own[5:6], zero], axis=1)
        arrived(got_v)
        flags = v_all[:, 0, :].astype(F32)
        flags = jnp.concatenate([flags, jnp.zeros((112, 128), F32)], axis=0).T
        lane = lax.broadcasted_iota(jnp.int32, (128, 64), 1)
        for blk in range(16):
            mask = (1.0 - flags[:, blk : blk + 1]) * NEG_FILL
            ext = jnp.where(lane == 0, mask, jnp.where(lane < 4, 1.0, 0.0))
            ka[blk * 128 : (blk + 1) * 128, 64:] = ext.astype(BF16)

    ext_lane = lax.broadcasted_iota(jnp.int32, (128, 64), 1)
    q_ext = jnp.where(ext_lane == 0, 1.0, 0.0).astype(BF16)
    v_ext = jnp.where(ext_lane < 3, 1.0, 0.0).astype(BF16)

    def project(slot):
        qkv = dot(nrm[slot], wq_use[...]) + ready["bias"]
        rows = pl.ds(pl.multiple_of(slot * 128, 128), 128)
        query = (qkv[:, :64].astype(BF16) * 0.125).astype(BF16)
        qa[rows, :] = jnp.concatenate([query, q_ext], axis=1)
        ka[rows, :64] = qkv[:, 64:128].astype(BF16)
        va[rows, :] = jnp.concatenate([qkv[:, 128:192].astype(BF16), v_ext], axis=1)

    gather.run(more_weights, prepare, project)
    grd[me.j] = (full_row(pv_all, 9) * gout[...].astype(F32)).astype(BF16)
    grad_gather = Gather8(wire, me, grd)
    grad_gather.start()

    heads_out = Scatter(me, as_, ar_, om, at)
    out_lane = lax.broadcasted_iota(jnp.int32, (256, 128), 1)

    def attend(k):
        chip = (me.chip + 1 + k) % 8
        rows = pl.ds(pl.multiple_of(chip * 256, 256), 256)
        scores = dot(qa[rows, :], ka[...], NT)
        row_max = jnp.max(scores, axis=1, keepdims=True)
        terms = jnp.exp(scores - row_max).astype(BF16)
        mixed = dot(terms, va[...])
        total = mixed[:, 64:65]
        heads = mixed / total
        log_sum = row_max + jnp.log(total)
        ow[rows, :] = jnp.where(out_lane < 64, heads, log_sum)
        rounded = heads[:, :64].astype(BF16)
        for e in range(2):
            om[chip * 2 + e] = fold(rounded[e * 128 : (e + 1) * 128])

    def attend_send(k, carry):
        attend(k)
        heads_out.send(k)
        return carry

    fan_w1.relay_near()
    fan_w2.relay_near()
    lax.fori_loop(0, 2, attend_send, 0)
    grad_gather.relay()
    fan_w1.relay_far()
    fan_w2.relay_far()
    lax.fori_loop(2, 5, attend_send, 0)
    grad_gather.middle()
    lax.fori_loop(5, 7, attend_send, 0)
    grad_gather.last()
    arrived(ready["wp"])
    swap = [wire.send(wp_all.at[f, half], wp_all.at[f, half], me.core) for f in range(8)]
    fan_wqf.start()
    attend(7)
    heads_out.keep(wire)
    heads_out.finish()

    attn_tok = jnp.concatenate([unfold(at[h]) for h in range(16)], axis=1)
    atg[me.j] = attn_tok
    arrived(swap)
    scale_one = full_row(pv_all, 8)
    branch = dot(attn_tok, wp_all[...].reshape(1024, 1024)) + full_row(pv_all, 6)
    middle = tok[...].astype(F32) + scale_one * branch
    mid[...] = middle
    normed, inverse = norm_stats(middle)
    gain = full_row(pv_all, 1)
    nmg[me.j] = (normed * gain + full_row(pv_all, 3)).astype(BF16)
    gather = Gather8(wire, me, nmg)
    gather.start()
    attn_gather = Gather8(wire, me, atg)
    grad_gather.finish()
    gather.relay()
    fan_w1.finish()
    fan_w2.finish()
    fan_wqf.relay_near()
    bias_one = jnp.concatenate(
        [pv_all[f].astype(F32)[10:11, :64] for f in range(8)], axis=1
    )
    reduce = Reduce8(wire, me, gn, r_core, r_far, r_near)

    def feed(b):
        two = pl.ds(2 * b, 2)
        rows = pl.ds(pl.multiple_of(b * 256, 256), 256)
        w1 = w1_all[...].reshape(1024, 512)
        w2 = w2_all[...].reshape(512, 1024)
        pre = dot(nmg[two].reshape(256, 1024), w1) + bias_one
        cdf = 0.5 * (1.0 + lax.erf(pre * 0.7071067811865476))
        acts = (pre * cdf).astype(BF16)
        act[rows, :] = acts
        mp[two] = dot(acts, w2).astype(BF16).reshape(2, 128, 1024)
        grad_act = dot(grd[two].reshape(256, 1024), w2, NT)
        slope = cdf + pre * jnp.exp(-0.5 * pre * pre) * 0.3989422804014327
        grad_pre = (grad_act * slope).astype(BF16)
        gpre[rows, :] = grad_pre
        gn[two] = dot(grad_pre, w1, NT).astype(BF16).reshape(2, 128, 1024)
        return column_sum(grad_pre.astype(F32))

    gather.cores[0].wait_recv()
    bias_sum = feed(me.y)
    reduce.start(3)
    gather.middle()
    attn_gather.start()
    gather.cores[1].wait_recv()
    bias_sum += feed(me.ym)
    reduce.start(2)
    gather.last()
    gather.cores[2].wait_recv()
    bias_sum += feed(me.yp)
    reduce.start(1)
    reduce.near_halves()
    gather.cores[3].wait_recv()
    db1[...] = bias_sum + feed(me.yo)
    reduce.start(0)
    fan_w1.settle()
    fan_w2.settle()
    fan_wqf.relay_far()
    reduce.far()
    attn_gather.relay()
    dw2[...] = dot(act[...], grd[...].reshape(1024, 1024), TN).astype(BF16).reshape(8, 64, 1024)
    reduce.near()
    fan_dw2 = FanIn(wire, me, dw2, r2)
    fan_dw2.start()
    dw1[...] = dot(nmg[...].reshape(1024, 1024), gpre[...], TN).astype(BF16).reshape(8, 128, 512)
    fan_dw1 = FanIn(wire, me, dw1, r1)
    fan_dw1.start()
    cotangent = reduce.result()
    grad_middle = gout[...].astype(F32) + norm_back(cotangent, gain, normed, inverse)
    gmid[...] = grad_middle
    grad_attn = (scale_one * grad_middle).astype(BF16)
    gat[...] = grad_attn
    grad_tok = dot(grad_attn, wp_all[...].reshape(1024, 1024), NT).astype(BF16)
    for h in range(16):
        msg[h] = fold(grad_tok[:, h * 64 : (h + 1) * 64])
    gh[me.s] = msg[me.s]
    got_gh = []
    for step in range(1, 16):
        peer = (me.s + step) % 16
        got_gh.append(wire.send(msg.at[peer], gh.at[me.s], (me.f, peer)))
    got_gac = []
    for step in range(1, 8):
        peer = (me.j + step) % 8
        device = (me.f, me.slot(peer // 2, me.xl, peer % 2))
        got_gac.append(wire.send(gat.at[:, lanes(peer * 128)], gac.at[me.j], device))
    gac[me.j] = gat[:, lanes(me.j * 128)]
    mlp = Reduce8(wire, me, mp, m_core, m_far, m_near)
    for d in range(4):
        mlp.start(d)
    zero = jnp.zeros((1, 1024), F32)
    vec[...] = jnp.concatenate(
        [
            zero,
            column_sum(cotangent * normed),
            zero,
            column_sum(cotangent),
            zero,
            zero,
            column_sum(grad_attn.astype(F32)),
            column_sum(grd[me.j].astype(F32)),
            column_sum(grad_middle * branch),
            jnp.zeros((7, 1024), F32),
        ],
        axis=0,
    )
    attn_gather.middle()
    attn_gather.last()
    mlp.far()
    mlp.near_halves()
    lane = lax.broadcasted_iota(jnp.int32, (128, 128), 1)
    for blk in range(16):
        rows = slice(blk * 128, (blk + 1) * 128)
        l1, l2, l3 = three_parts(-ow[rows, 64:65])
        wide = qa[rows, :].astype(F32)
        wide = jnp.where(lane == 65, l1, wide)
        wide = jnp.where(lane == 66, l2, wide)
        wide = jnp.where(lane == 67, l3, wide)
        qb[rows, :] = wide.astype(BF16)
        kt[:, rows] = ka[rows, :].astype(F32).T.astype(BF16)
    for f in range(8):
        weight = wq_all[f].astype(F32)
        wqt[f, :128] = weight[:, :128].T.astype(BF16)
        wqt[f, 128:] = weight[:, 128:].T[:64].astype(BF16)
    dk[...] = jnp.zeros_like(dk)
    dv[...] = jnp.zeros_like(dv)

    arrived(got_gh)
    for blk in range(16):
        rows = slice(blk * 128, (blk + 1) * 128)
        grad = unfold(gh[blk])
        delta = jnp.sum(grad.astype(F32) * ow[rows, :64], axis=1, keepdims=True)
        d1, d2, d3 = three_parts(-delta)
        wide = jnp.concatenate([grad, jnp.zeros((128, 64), BF16)], axis=1).astype(F32)
        wide = jnp.where(lane == 64, d1, wide)
        wide = jnp.where(lane == 65, d2, wide)
        wide = jnp.where(lane == 66, d3, wide)
        ga[rows, :] = wide.astype(BF16)

    queries_out = Scatter(me, bs, br, qm, qin)

    def back(k):
        chip = (me.chip + 1 + k) % 8
        rows = pl.ds(pl.multiple_of(chip * 256, 256), 256)
        query, grad = qb[rows, :], ga[rows, :]
        probs = jnp.exp(dot(ka[...], query, NT))
        dv[...] += dot(probs.astype(BF16), grad)
        slope = dot(va[...], grad, NT)
        scores = (probs * slope).astype(BF16)
        dk[...] += dot(scores, query)
        turned = dot(kt[...], scores)
        grad_query = (turned.T[:, :64] * 0.125).astype(BF16)
        dqt[:64, rows] = (turned[:64] * 0.125).astype(BF16)
        for e in range(2):
            qm[chip * 2 + e] = fold(grad_query[e * 128 : (e + 1) * 128])

    def back_send(k, carry):
        back(k)
        queries_out.send(k)
        return carry

    lax.fori_loop(0, 3, back_send, 0)
    mlp.near()
    arrived(got_gac)
    attn_gather.finish()
    for f in range(8):
        tok_cols = atg[:, :, f * 128 : (f + 1) * 128].reshape(1024, 128)
        dwp[f] = dot(tok_cols, gac[...].reshape(1024, 128), TN).astype(BF16)
    fan_dw2.forward()
    fan_dw1.forward()
    got = to_fsdp(wire, me, lambda p: dwp.at[p], lambda f: rp.at[f])
    rp[me.f] = dwp[me.f]
    lax.fori_loop(3, 6, back_send, 0)
    fan_wqf.finish()
    swap = [wire.send(wqf.at[f, half], wqf.at[f, half], me.core) for f in range(8)]
    lax.fori_loop(6, 7, back_send, 0)
    back(7)
    queries_out.keep(wire)

    for blk in range(16):
        rows = slice(blk * 128, (blk + 1) * 128)
        grad_key, grad_value = dk[rows, :64].astype(BF16), dv[rows, :64].astype(BF16)
        pair = jnp.concatenate([grad_key, grad_value], axis=1)
        kvm[blk] = pair
        dqt[64:, rows] = pair.astype(F32).T.astype(BF16)
    got_kv = []
    for step in range(1, 16):
        peer = (me.s + step) % 16
        got_kv.append(wire.send(kvm.at[peer], kvin.at[me.s], (me.f, peer)))
    kvin[me.s] = kvm[me.s]

    arrived(got)
    x1[0] = fan_dw1.result().astype(BF16)
    x2[0] = fan_dw2.result().astype(BF16)
    xp[0] = eight(rp).astype(BF16)
    crossed = [wire.send(x.at[0], x.at[1], me.xpart) for x in (x1, x2, xp)]
    mlp_out = mlp.result() + full_row(pv_all, 7)
    res[...] = (mid[...] + full_row(pv_all, 9) * mlp_out).astype(BF16)
    vec[9:10, :] = column_sum(gout[...].astype(F32) * mlp_out)
    sums = jnp.sum(dqt[...].astype(F32), axis=1, keepdims=True)
    turned = jnp.broadcast_to(sums, (192, 128))
    turned = jnp.concatenate([turned, jnp.zeros((64, 128), F32)], axis=0)
    sum_q, sum_v = turned[:128].T[0:1, :64], turned[128:].T[0:1, :64]
    got_q, got_vec = [], []
    for step in range(1, 9):
        f = (me.f + step) % 8
        own = pv_all[f].astype(F32)
        product = dot(dqt[...], nrm[:, :, lanes(f * 128)].reshape(2048, 128))
        grad_wq = product * own[0:1] + sums * own[2:3]
        weight = wqt[f].astype(F32)
        rows = vec[:, lanes(f * 128)]
        piece = half_of(f % 2, db1[:, lanes((f // 2) * 128)])
        bias = beside(me.c, piece)
        here = me.chip == f
        packed = jnp.concatenate(
            [
                column_sum(weight * product),
                rows[1:2],
                column_sum(weight * sums),
                rows[3:4],
                jnp.where(here, beside(me.c, sum_q), 0.0),
                jnp.where(here, beside(me.c, sum_v), 0.0),
                rows[6:10],
                *[jnp.where(me.y == y, bias, 0.0) for y in range(4)],
                jnp.zeros((2, 128), F32),
            ],
            axis=0,
        )
        if step < 8:
            dwq[f] = grad_wq.astype(BF16)
            vs[f] = packed
            got_q.append(wire.send(dwq.at[f], rq.at[me.f], (f, me.s)))
            got_vec.append(wire.send(vs.at[f], vr.at[me.f], (f, me.s)))
        else:
            rq[me.f] = grad_wq.astype(BF16)
            vr[me.f] = packed

    arrived(crossed)
    gathers = []
    for x, g in ((x1, w1_all), (x2, w2_all), (xp, gp)):
        g[me.j] = (x[0].astype(F32) + x[1].astype(F32)).astype(BF16)
        gathers.append(Gather8(wire, me, g))
    for gather in gathers:
        gather.start()

    queries_out.finish()
    arrived(got_kv)
    arrived(swap)
    parts = [unfold(qin[h]) for h in range(16)]
    parts += [kvin[h][:, :64] for h in range(16)] + [kvin[h][:, 64:] for h in range(16)]
    grad_qkv = jnp.concatenate(parts, axis=1)
    cotangent = dot(grad_qkv, wqf[...].reshape(1024, 3072), NT)

    arrived(got_q)
    gq[me.s] = eight(rq).astype(BF16)
    gather_q = Gather16(wire, me, gq)
    gather_q.start()
    arrived(got_vec)
    vq[me.s] = eight(vr)
    got_vq = []
    for step in range(1, 16):
        peer = (me.s + step) % 16
        got_vq.append(wire.send(vq.at[me.s], vq.at[me.s], (me.f, peer)))
    for gather in gathers:
        gather.relay()
    for gather in gathers:
        gather.middle()
    normed, inverse = norm_stats(tok[...].astype(F32))
    gtok[...] = gmid[...] + norm_back(cotangent, full_row(pv_all, 0), normed, inverse)
    for gather in gathers:
        gather.last()
    gather_q.run()
    for gather in gathers:
        gather.finish()
    arrived(got_vq)
    total = vq[0]
    for s in range(1, 16):
        total = total + vq[s]
    o_vec[...] = total
    wire.drain()


OUTS = (
    ((128, 1024), BF16),
    ((128, 1024), F32),
    ((16, 192, 128), BF16),
    ((8, 128, 128), BF16),
    ((8, 128, 512), BF16),
    ((8, 64, 1024), BF16),
    ((16, 128), F32),
)
GRADS = (
    ((128, 1024), BF16),
    ((128, 1024), F32),
    ((128, 3072), F32),
    ((128, 1024), F32),
    ((128, 4096), F32),
    ((512, 1024), F32),
    ((2, 128), F32),
    ((6, 128), F32),
    ((2, 128), F32),
    ((1, 512), F32),
)


def lay_out(*refs):
    count = len(OUTS)
    given, outs = refs[:count], refs[count : count + len(GRADS)]
    scratch, sem = refs[count + len(GRADS) : -1], refs[-1]
    held, ready = scratch[:count], scratch[count:]
    copies = []
    for k in (5, 4, 2, 3, 6, 0, 1):
        copies.append(pltpu.make_async_copy(given[k], held[k], sem.at[k]))
        copies[-1].start()

    def store(k):
        src = held[k] if k < 2 else ready[k - 2]
        copies.append(pltpu.make_async_copy(src, outs[k], sem.at[count + k]))
        copies[-1].start()

    gq, gp, g1, g2, vec = held[2:]
    o_qkv, o_proj, o_fc1, o_fc2 = ready[:4]
    copies[0].wait()
    for j in range(8):
        o_fc2[j * 64 : (j + 1) * 64, :] = g2[j].astype(F32)
    store(5)
    copies[1].wait()
    for f in range(8):
        cols = slice(f * 64, (f + 1) * 64)
        for k in range(4):
            pair = jnp.concatenate([g1[2 * k, :, cols], g1[2 * k + 1, :, cols]], axis=1)
            at = f * 512 + k * 128
            o_fc1[:, at : at + 128] = pair.astype(F32)
    store(4)
    copies[2].wait()
    for part in range(3):
        rows = slice(part * 64, (part + 1) * 64)
        for k in range(8):
            pair = jnp.concatenate([gq[2 * k, rows, :], gq[2 * k + 1, rows, :]], axis=0)
            at = part * 1024 + k * 128
            o_qkv[:, at : at + 128] = pair.astype(F32).T
    store(2)
    copies[3].wait()
    for j in range(8):
        o_proj[:, j * 128 : (j + 1) * 128] = gp[j].astype(F32)
    store(3)
    copies[4].wait()
    row = 0
    for k in range(6, 9):
        size = GRADS[k][0][0]
        ready[k - 2][...] = vec[row : row + size, :]
        row += size
        store(k)
    ready[7][...] = jnp.concatenate([vec[k : k + 1, :] for k in range(row, row + 4)], axis=1)
    store(9)
    for k in (0, 1):
        copies[5 + k].wait()
        store(k)
    for copy in copies[7:]:
        copy.wait()


SCRATCH = (
    ((16, 128, 1024), BF16),
    ((8, 128, 1024), BF16),
    ((8, 16, 128), BF16),
    ((16, 16, 128), BF16),
    ((128, 256), BF16),
    ((8, 128, 256), BF16),
    ((1024, 256), BF16),
    ((8, 128, 1024), BF16),
    ((128, 512), BF16),
    ((8, 128, 3072), BF16),
    ((2048, 128), BF16),
    ((2048, 128), BF16),
    ((2048, 128), BF16),
    ((2048, 128), F32),
    ((16, 64, 128), BF16),
    ((16, 64, 128), BF16),
    ((8, 128, 1024), BF16),
    ((1024, 512), BF16),
    ((1024, 512), BF16),
    ((8, 128, 1024), BF16),
    ((8, 128, 1024), BF16),
    ((4, 128, 1024), BF16),
    ((2, 64, 1024), BF16),
    ((2, 128, 1024), BF16),
    ((16, 64, 128), BF16),
    ((128, 1024), BF16),
    ((128, 1024), F32),
    ((128, 1024), F32),
    ((8, 128, 1024), BF16),
    ((8, 128, 128), BF16),
    ((16, 64, 128), BF16),
    ((8, 128, 512), BF16),
    ((8, 64, 1024), BF16),
    ((16, 1024), F32),
    ((1, 512), F32),
    ((2048, 128), BF16),
    ((2048, 128), BF16),
    ((128, 2048), BF16),
    ((2048, 128), F32),
    ((2048, 128), F32),
    ((192, 2048), BF16),
    ((8, 192, 128), BF16),
    ((16, 64, 128), BF16),
    ((16, 64, 128), BF16),
    ((16, 128, 128), BF16),
    ((16, 128, 128), BF16),
    ((4, 128, 1024), BF16),
    ((2, 64, 1024), BF16),
    ((2, 128, 1024), BF16),
    ((8, 128, 128), BF16),
    ((8, 128, 512), BF16),
    ((8, 64, 1024), BF16),
    ((8, 128, 128), BF16),
    ((2, 128, 512), BF16),
    ((2, 64, 1024), BF16),
    ((2, 128, 128), BF16),
    ((8, 192, 128), BF16),
    ((8, 192, 128), BF16),
    ((8, 16, 128), F32),
    ((8, 16, 128), F32),
    ((16, 16, 128), F32),
)
COPIES = 352


def body(
    tokens, image_ids, valid, w_qkv, w_proj, w_fc1, w_fc2,
    norm_gain, shifts, layer_scale, fc1_bias, grad_out,
):
    semaphores = [pltpu.SemaphoreType.DMA((n,)) for n in (COPIES, COPIES, 14, 14, 14, 14, 2)]
    whole = pl.BlockSpec(memory_space=pltpu.VMEM)
    held = pl.BlockSpec(memory_space=pl.ANY)
    shares = pl.pallas_call(
        layer,
        out_shape=[jax.ShapeDtypeStruct(shape, dtype) for shape, dtype in OUTS],
        in_specs=[whole] * 4 + [held, whole, held] + [whole] * 4,
        out_specs=[whole] * len(OUTS),
        scratch_shapes=[pltpu.VMEM(shape, dtype) for shape, dtype in SCRATCH] + semaphores,
        name="layer",
        compiler_params=pltpu.CompilerParams(
            collective_id=1, has_side_effects=True, vmem_limit_bytes=VMEM_LIMIT
        ),
    )(
        tokens, grad_out, valid.reshape(1, 128), w_qkv[0], w_proj[0], w_fc1[0], w_fc2[0],
        norm_gain[0], shifts[0], layer_scale[0], fc1_bias,
    )
    outs = pl.pallas_call(
        lay_out,
        out_shape=[jax.ShapeDtypeStruct(shape, dtype) for shape, dtype in GRADS],
        in_specs=[held] * len(OUTS),
        out_specs=[held] * len(GRADS),
        scratch_shapes=[pltpu.VMEM(shape, dtype) for shape, dtype in OUTS + GRADS[2:]]
        + [pltpu.SemaphoreType.DMA((len(OUTS) + len(GRADS),))],
        name="lay_out",
        compiler_params=pltpu.CompilerParams(vmem_limit_bytes=VMEM_LIMIT),
    )(*shares)
    return (*outs[:2], *[out[None] for out in outs[2:9]], outs[9])


def solution(mesh):
    rows = P(("fsdp", "seq"), None)
    flat = P(("fsdp", "seq"))
    mats = P(None, "fsdp", None)
    vecs = P(None, None, "fsdp")
    bias = P(None, "fsdp")
    return jax.shard_map(
        body,
        mesh=mesh,
        in_specs=(rows, flat, flat, mats, mats, mats, mats, vecs, vecs, vecs, bias, rows),
        out_specs=(rows, rows, mats, mats, mats, mats, vecs, vecs, vecs, bias),
        check_vma=False,
    )
```
